128 devices in a mesh: batch: 16 (over y, z_lo, core), seq: 8 (over x, z_hi).
Axes of the slice: x: 4, y: 4, z: 4 (z_hi: 2, z_lo: 2; z = z_hi * 2 + z_lo), core: 2. Of those that a mesh axis runs over, the one named last changes fastest.
Arguments:
- block_input: bfloat16 [16, 1024, 1536], P('batch', 'seq'), may hold values from -6 to 6
- doc_lengths: int32 [16, 6], P('batch'), may hold values from 1 to 1019, as said below
- ffn_levels: int32 [16, 6], P('batch'), may hold values from 0 to 3
- attn_gain: bfloat16 [1536], P(('batch', 'seq')), may hold values from 0.5 to 1.5
- qkv_weight: bfloat16 [1536, 4608], P(('batch', 'seq')), may hold values from -0.15625 to 0.15625
- out_weight: bfloat16 [1536, 1536], P(('batch', 'seq')), may hold values from -0.875 to 0.875
- ffn_gain: bfloat16 [1536], P(('batch', 'seq')), may hold values from 0.5 to 1.5
- up_weight: bfloat16 [1536, 6144], P(('batch', 'seq')), may hold values from -0.15625 to 0.15625
- down_weight: bfloat16 [6144, 1536], P(('batch', 'seq')), may hold values from -0.109375 to 0.109375
- grad_output: bfloat16 [16, 1024, 1536], P('batch', 'seq'), may hold values from -6 to 6
Outputs:
- block_output: bfloat16 [16, 1024, 1536], P('batch', 'seq')
- grad_input: float32 [16, 1024, 1536], P('batch', 'seq')
- grad_attn_gain: float32 [1536], P(('batch', 'seq'))
- grad_qkv: float32 [1536, 4608], P(('batch', 'seq'))
- grad_out: float32 [1536, 1536], P(('batch', 'seq'))
- grad_ffn_gain: float32 [1536], P(('batch', 'seq'))
- grad_up: float32 [1536, 6144], P(('batch', 'seq'))
- grad_down: float32 [6144, 1536], P(('batch', 'seq'))
The draws below stay inside these ranges and needn't reach their ends.
Inputs may be any that keep to these rules, and one draw needn't show every extreme that they name: `doc_lengths`: in each group the 6 lengths sum to 1024; one of them, in a slot drawn from the seed, is longer than all the others together, and each of the others holds 1 to 16 tokens; in one group, drawn from the seed, each of the others holds exactly 1 token.
All inputs are finite; a program needn't handle non-finite values.
Results may differ from the reference program's by a relative error of at most 0.019.
Values may be sent and summed in bfloat16 or wider, within the bound.
A program may use at most 320 MiB of HBM per device.

```python
import math
import jax
import jax.numpy as jnp
from jax import lax

HEADS = 12
HEAD_DIM = 128
D = 1536
FF = 6144
DOCS = 6
GROUP = 1024
SHARD = 128
GROUPS = 16


def draw_doc_lengths(key, part):
    key = jax.random.fold_in(key, 11)
    short_key, slot_key, group_key = jax.random.split(key, 3)
    short_rows = jax.random.randint(short_key, (GROUPS, DOCS), 1, SHARD // 8 + 1)
    least_group = jax.random.randint(group_key, (), 0, GROUPS)
    in_least = (jnp.arange(GROUPS, dtype=jnp.int32) == least_group)[:, None]
    short_rows = jnp.where(in_least, 1, short_rows)
    long_slot = jax.random.randint(slot_key, (GROUPS, 1), 0, DOCS)
    is_long = jnp.arange(DOCS, dtype=jnp.int32)[None, :] == long_slot
    short_rows = jnp.where(is_long, 0, short_rows)
    long_rows = GROUP - jnp.sum(short_rows, axis=1, keepdims=True)
    return jnp.where(is_long, long_rows, short_rows).astype(jnp.int32)


def with_ends(array, own_key, least, top_value):
    index_at = [jax.random.randint(jax.random.fold_in(own_key, axis), (), 0, length) for axis, length in enumerate(array.shape)]
    main_axis = array.shape.index(max(array.shape))
    beside = index_at[:main_axis] + [(index_at[main_axis] + 1) % array.shape[main_axis]] + index_at[main_axis + 1:]
    return array.at[tuple(index_at)].set(least).at[tuple(beside)].set(top_value)


def block_levels(stream_key, extent, shards, smallest, largest):
    def one(position, shards_of):
        heights = jax.random.uniform(jax.random.fold_in(jax.random.fold_in(stream_key, 6), position), (shards_of,), jnp.float32, smallest / len(shards), largest / len(shards))
        return jnp.repeat(jnp.exp(heights), extent[position] // shards_of).reshape((-1,) + (1,) * (len(extent) - position - 1))

    factor_of = one(*shards[0])
    for cut in shards[1:]:
        factor_of = factor_of * one(*cut)
    return factor_of


def gaussian(stream_key, dims, scale, limit, cuts=(), held_as=jnp.bfloat16):
    factor_of = block_levels(stream_key, dims, cuts, -0.22, 0.18) if cuts else 1.0
    drawn = jax.random.normal(stream_key, dims, jnp.float32) * scale * factor_of
    return jnp.minimum(jnp.maximum(drawn, -limit), limit).astype(held_as)


def setup_inputs(seed: int = 0) -> dict:
    splits = jax.random.split(jax.random.key(seed), 11)
    return {
        "block_input": gaussian(splits[0], (GROUPS, GROUP, D), 1.0, 6.0, ((0, 16), (1, 8))),
        "doc_lengths": draw_doc_lengths(jax.random.fold_in(splits[10], 71), 0),
        "ffn_levels": with_ends(jax.random.randint(splits[2], (GROUPS, DOCS), 0, 4), jax.random.fold_in(splits[2], 1), 0, 3).astype(jnp.int32),
        "attn_gain": jnp.clip(1.0 + 0.1 * jax.random.normal(splits[3], (D,), jnp.float32), 0.5, 1.5).astype(jnp.bfloat16),
        "qkv_weight": gaussian(splits[4], (D, 3 * D), D ** -0.5, 0.15625, ((0, 128),)),
        "out_weight": gaussian(splits[5], (D, D), (max(1, D // 32)) ** -0.5, 0.875, ((0, 128),)),
        "ffn_gain": jnp.clip(1.0 + 0.1 * jax.random.normal(splits[6], (D,), jnp.float32), 0.5, 1.5).astype(jnp.bfloat16),
        "up_weight": gaussian(splits[7], (D, FF), D ** -0.5, 0.15625, ((0, 128),)),
        "down_weight": gaussian(splits[8], (FF, D), (FF // 2) ** -0.5, 0.109375, ((0, 128),)),
        "grad_output": gaussian(splits[9], (GROUPS, GROUP, D), 1.0, 6.0, ((0, 16), (1, 8))),
    }


@jax.custom_vjp
def low(v):
    return lax.optimization_barrier(v.astype(jnp.bfloat16)).astype(jnp.float32)

@jax.custom_vjp
def low_back(v):
    return v

def low_keep(v):
    return (low(v), None)

def low_pass(kept, grad):
    return (grad,)

def back_keep(v):
    return (v, None)

def back_low(kept, grad):
    return (low(grad),)
low.defvjp(low_keep, low_pass)
low_back.defvjp(back_keep, back_low)
epsilon = 1e-06
precise = lax.Precision.HIGHEST

def rms_scale(values, gain):
    return values * lax.rsqrt(lax.optimization_barrier(jnp.mean(values * values, axis=-1, keepdims=True)) + epsilon) * gain

def rotary_tables(offsets):
    half_dim = HEAD_DIM // 2
    inverse = jnp.exp(jnp.arange(half_dim, dtype=jnp.float32) * (-2.0 * math.log(10000.0) / HEAD_DIM))
    angles = offsets.astype(jnp.float32)[:, None] * inverse[None, :]
    cosines = jnp.concatenate([jnp.cos(angles), jnp.cos(angles)], axis=-1)
    sines = jnp.concatenate([jnp.sin(angles), jnp.sin(angles)], axis=-1)
    return (cosines, sines)

def rotate(heads_in, cosines, sines):
    half_dim = HEAD_DIM // 2
    turned = jnp.concatenate([-heads_in[..., half_dim:], heads_in[..., :half_dim]], axis=-1)
    return heads_in * cosines[:, None, :] + turned * sines[:, None, :]

def layout(lengths, levels, positions):
    doc_ends = jnp.cumsum(lengths).astype(jnp.int32)
    doc_starts = doc_ends - lengths
    doc_ids = lax.optimization_barrier(jnp.sum((positions[:, None] >= doc_ends[None, :]).astype(jnp.int32), axis=1))
    one_hot = (doc_ids[:, None] == jnp.arange(DOCS, dtype=jnp.int32)[None, :]).astype(jnp.int32)
    offsets = positions - lax.optimization_barrier(jnp.sum(one_hot * doc_starts[None, :], axis=1))
    widths = lax.optimization_barrier(jnp.sum(one_hot * (FF // 8 * jnp.power(2, levels))[None, :], axis=1))
    return (doc_ids, offsets, widths)

def attention(queries, key_rows, value_rows, doc_ids):
    block_rows = min(512, GROUP)
    key_positions = jnp.arange(GROUP, dtype=jnp.int32)
    score_scale = HEAD_DIM ** (-0.5)

    def one_block(block_index):
        first = (block_index * block_rows).astype(jnp.int32)
        query_block = lax.dynamic_slice_in_dim(queries, first, block_rows, 0)
        doc_block = lax.dynamic_slice_in_dim(doc_ids, first, block_rows, 0)
        query_positions = first + jnp.arange(block_rows, dtype=jnp.int32)
        scores = jnp.einsum('qhd,khd->hqk', query_block, key_rows, precision=precise) * score_scale
        scores = low_back(scores)
        allowed = (doc_block[:, None] == doc_ids[None, :]) & (key_positions[None, :] <= query_positions[:, None])
        scores = jnp.where(allowed[None], scores, -1e+30)
        probs = low(jax.nn.softmax(scores, axis=-1))
        return jnp.einsum('hqk,khd->qhd', probs, value_rows, precision=precise)
    blocks = lax.map(jax.checkpoint(one_block), jnp.arange(GROUP // block_rows, dtype=jnp.int32))
    return blocks.reshape(GROUP, HEADS * HEAD_DIM)

def reference(block_input, doc_lengths, ffn_levels, attn_gain, qkv_weight, out_weight, ffn_gain, up_weight, down_weight, grad_output):
    positions = jnp.arange(GROUP, dtype=jnp.int32)
    model_width = HEADS * HEAD_DIM

    def forward(inputs, gain_one, weight_qkv, weight_out, gain_two, weight_up, weight_down):

        def one_group(packed):
            group_rows, lengths, levels = packed
            doc_ids, offsets, widths = layout(lengths, levels, positions)
            cosines, sines = rotary_tables(offsets)
            normed = low(rms_scale(group_rows, gain_one))
            projected = low_back(jnp.dot(normed, weight_qkv, precision=precise))
            queries = projected[:, :model_width].reshape(GROUP, HEADS, HEAD_DIM)
            key_rows = projected[:, model_width:2 * model_width].reshape(GROUP, HEADS, HEAD_DIM)
            value_rows = projected[:, 2 * model_width:].reshape(GROUP, HEADS, HEAD_DIM)
            queries = low(rotate(queries, cosines, sines))
            key_rows = low(rotate(key_rows, cosines, sines))
            value_rows = low(value_rows)
            attended = low_back(low(attention(queries, key_rows, value_rows, doc_ids)))
            branch = low_back(jnp.dot(attended, weight_out, precision=precise))
            middle = group_rows + branch
            normed_two = low(rms_scale(middle, gain_two))
            pre_gelu = low_back(jnp.dot(normed_two, weight_up, precision=precise))
            unit_mask = (jnp.arange(FF, dtype=jnp.int32)[None, :] < widths[:, None]).astype(jnp.float32)
            hidden = low(jax.nn.gelu(pre_gelu) * unit_mask)
            return middle + jnp.dot(hidden, weight_down, precision=precise)
        return lax.map(jax.checkpoint(one_group), (inputs, doc_lengths, ffn_levels))
    floats = (block_input.astype(jnp.float32), attn_gain.astype(jnp.float32), qkv_weight.astype(jnp.float32), out_weight.astype(jnp.float32), ffn_gain.astype(jnp.float32), up_weight.astype(jnp.float32), down_weight.astype(jnp.float32))
    outputs, pull_back = jax.vjp(forward, *floats)
    grads = pull_back(grad_output.astype(jnp.float32))
    return (outputs.astype(jnp.bfloat16), grads[0], grads[1], grads[2], grads[3], grads[4], grads[5], grads[6])
```

```python
import math

import jax
import jax.numpy as jnp
from jax import lax
from jax.experimental import pallas as pl
from jax.experimental.pallas import tpu as pltpu
from jax.sharding import PartitionSpec as P

HEADS = 12
HEAD_DIM = 128
D = 1536
FF = 6144
DOCS = 6
GROUP = 1024
SHARD = 128
RANK_HEADS = 3
RANK_COLS = 384
EPS = 1e-06
BF = jnp.bfloat16
F32 = jnp.float32
MESH = pl.DeviceIdType.MESH


def coords():
    b = lax.axis_index("batch")
    s = lax.axis_index("seq")
    return b // 4, (b // 2) % 2, b % 2, s // 2, s % 2


def dev(y, zl, c, x, zh):
    return (y * 4 + zl * 2 + c, x * 2 + zh)


def barrier(peers):
    sem = pltpu.get_barrier_semaphore()
    for peer in peers:
        pl.semaphore_signal(sem, inc=1, device_id=peer, device_id_type=MESH)
    pl.semaphore_wait(sem, len(peers))


def x_peers():
    y, zl, c, x, zh = coords()
    return [dev(y, zl, c, (x + k) % 4, zh) for k in (1, 2, 3)]


def y_peers():
    y, zl, c, x, zh = coords()
    return [dev((y + k) % 4, zl, c, x, zh) for k in (1, 2, 3)]


def z_peers():
    y, zl, c, x, zh = coords()
    z = zh * 2 + zl
    return [dev(y, (z + k) % 2, c, x, ((z + k) % 4) // 2) for k in (1, 2, 3)]


def core_peer():
    y, zl, c, x, zh = coords()
    return dev(y, zl, 1 - c, x, zh)


def zh_peer():
    y, zl, c, x, zh = coords()
    return dev(y, zl, c, x, 1 - zh)


class Lines:
    def __init__(self, send, recv):
        self.send, self.recv, self.used = send, recv, 0

    def copy(self, src, dst, peer):
        at = self.used
        self.used += 1
        return pltpu.make_async_remote_copy(
            src, dst, self.send.at[at], self.recv.at[at], device_id=peer, device_id_type=MESH
        )


LO, HI = pl.ds(0, 64), pl.ds(64, 64)


def ring_gather(lines, slot):
    x = coords()[3]
    nxt, _, prv = x_peers()
    left, right = (x + 3) % 4, (x + 1) % 4
    first = lines.copy(slot(x).at[LO], slot(x).at[LO], nxt)
    second = lines.copy(slot(x).at[HI], slot(x).at[HI], prv)
    third = lines.copy(slot(x).at[HI], slot(x).at[HI], nxt)
    fourth = lines.copy(slot(x).at[LO], slot(x).at[LO], prv)
    for cp in (first, second, third, fourth):
        cp.start()
    first.wait_recv()
    on = lines.copy(slot(left).at[LO], slot(left).at[LO], nxt)
    on.start()
    second.wait_recv()
    back = lines.copy(slot(right).at[HI], slot(right).at[HI], prv)
    back.start()

    def finish():
        first.wait_send()
        second.wait_send()
        for cp in (third, fourth, on, back):
            cp.wait()

    return finish


def ring_scatter(lines, part, got, on_buf):
    x = coords()[3]
    nxt, _, prv = x_peers()
    left, right, far = (x + 3) % 4, (x + 1) % 4, (x + 2) % 4
    far_lo = lines.copy(part(far).at[LO], on_buf.at[0], nxt)
    far_hi = lines.copy(part(far).at[HI], on_buf.at[1], prv)
    near_hi = lines.copy(part(right).at[HI], got.at[2], nxt)
    near_lo = lines.copy(part(left).at[LO], got.at[0], prv)
    for cp in (far_lo, far_hi, near_hi, near_lo):
        cp.start()
    far_lo.wait_recv()
    on_buf[2] = (on_buf[0].astype(F32) + part(right)[LO].astype(F32)).astype(BF)
    on = lines.copy(on_buf.at[2], got.at[1], nxt)
    on.start()
    far_hi.wait_recv()
    on_buf[3] = (on_buf[1].astype(F32) + part(left)[HI].astype(F32)).astype(BF)
    back = lines.copy(on_buf.at[3], got.at[3], prv)
    back.start()

    def finish():
        far_lo.wait_send()
        far_hi.wait_send()
        for cp in (near_hi, near_lo, on, back):
            cp.wait()

    return finish


def ring_total(got):
    lo = got[0].astype(F32) + got[1].astype(F32)
    hi = got[2].astype(F32) + got[3].astype(F32)
    return jnp.concatenate([lo, hi], axis=0)


def gather_x_kernel(a, out, send, recv):
    x = coords()[3]
    barrier(x_peers()[::2])
    out[x] = a[...]
    ring_gather(Lines(send, recv), lambda i: out.at[i])()


def gather_seq_kernel(a, out, send, recv):
    _, _, _, x, zh = coords()
    barrier(x_peers()[::2] + [zh_peer()])
    lines = Lines(send, recv)
    out[x * 2 + zh] = a[...]
    swap = lines.copy(out.at[x * 2 + zh], out.at[x * 2 + zh], zh_peer())
    swap.start()
    done = ring_gather(lines, lambda i: out.at[i * 2 + zh])
    swap.wait_recv()
    done_too = ring_gather(lines, lambda i: out.at[i * 2 + 1 - zh])
    swap.wait_send()
    done()
    done_too()


def scatter_x_kernel(parts, out, got, on_buf, send, recv):
    x = coords()[3]
    barrier(x_peers()[::2])
    ring_scatter(Lines(send, recv), lambda i: parts.at[i], got, on_buf)()
    out[...] = parts[x].astype(F32) + ring_total(got)


def scatter_seq_kernel(parts, out, got, on_buf, got_too, on_too, swap_out, swap_in, send, recv):
    _, _, _, x, zh = coords()
    barrier(x_peers()[::2] + [zh_peer()])
    lines = Lines(send, recv)
    done_too = ring_scatter(lines, lambda i: parts.at[i * 2 + 1 - zh], got_too, on_too)
    done = ring_scatter(lines, lambda i: parts.at[i * 2 + zh], got, on_buf)
    done_too()
    swap_out[...] = (parts[x * 2 + 1 - zh].astype(F32) + ring_total(got_too)).astype(BF)
    swap = lines.copy(swap_out, swap_in, zh_peer())
    swap.start()
    done()
    swap.wait()
    out[...] = parts[x * 2 + zh].astype(F32) + ring_total(got) + swap_in[...].astype(F32)


def one_hot_rows(rows, cols, expand):
    i = lax.broadcasted_iota(jnp.int32, (rows, cols), 0)
    j = lax.broadcasted_iota(jnp.int32, (rows, cols), 1)
    a, p = (j, i) if expand else (i, j)
    return jnp.where((p % 16 < 12) & (p // 16 * 12 + p % 16 == a), 1.0, 0.0).astype(BF)


def pick(matrix, values):
    return jnp.dot(matrix, values, preferred_element_type=F32).astype(BF)


def seq_peers():
    y, zl, c, x, zh = coords()
    s = x * 2 + zh
    found = []
    for k in range(1, 8):
        t = (s + k) % 8
        found.append(dev(y, zl, c, t // 2, t % 2))
    return found


def weight_peers():
    return seq_peers() + y_peers() + z_peers()[::2] + [core_peer()]


def swap_xy():
    y, zl, c, x, zh = coords()
    return dev(x, zl, c, y, zh)


def all_weight_barrier():
    y, _, _, x, _ = coords()
    sem = pltpu.get_barrier_semaphore()
    peers = weight_peers()
    for peer in peers:
        pl.semaphore_signal(sem, inc=1, device_id=peer, device_id_type=MESH)

    @pl.when(x != y)
    def _():
        pl.semaphore_signal(sem, inc=1, device_id=swap_xy(), device_id_type=MESH)

    pl.semaphore_wait(sem, len(peers) + jnp.where(x != y, 1, 0))


def spread(lines, src, dst):
    y, zl, c, x, zh = coords()
    s = x * 2 + zh
    at = lines.used
    lines.used += 4
    sends, arrivals = [], []
    for k in range(4):
        i = (x + k) % 4
        own = (i == x) & (x // 2 == zh)
        cp = pltpu.make_async_remote_copy(
            src.at[i], dst.at[s % 4], lines.send.at[at + k], lines.recv.at[at + s % 4],
            device_id=dev(y, zl, c, i, x // 2), device_id_type=MESH,
        )
        sends.append((cp, own))
    for j in range(4):
        own = (x // 2 == zh) & (s % 4 == j)
        cp = pltpu.make_async_remote_copy(
            src.at[j], dst.at[j], lines.send.at[at], lines.recv.at[at + j],
            device_id=core_peer(), device_id_type=MESH,
        )
        arrivals.append((cp, own))
    return sends, arrivals, (x // 2 == zh), x, s % 4


def gather_home(lines, src, dst):
    y, zl, c, x, zh = coords()
    s = x * 2 + zh
    at = lines.used
    lines.used += 4
    sends, arrivals = [], []
    for k in range(4):
        i = (s + k) % 4
        t = 4 * zh + i
        own = t == s
        cp = pltpu.make_async_remote_copy(
            src.at[i], dst.at[x], lines.send.at[at + k], lines.recv.at[at + x],
            device_id=dev(y, zl, c, t // 2, t % 2), device_id_type=MESH,
        )
        sends.append((cp, own))
    for j in range(4):
        own = (x // 2 == zh) & (x == j)
        cp = pltpu.make_async_remote_copy(
            src.at[j], dst.at[j], lines.send.at[at], lines.recv.at[at + j],
            device_id=core_peer(), device_id_type=MESH,
        )
        arrivals.append((cp, own))
    return sends, arrivals, (x // 2 == zh), s % 4, x


def start_all(plan, src, dst):
    sends, _, mine, from_slot, to_slot = plan
    for cp, own in sends:
        pl.when(jnp.logical_not(own))(cp.start)

    @pl.when(mine)
    def _():
        dst[to_slot] = src[from_slot]


def wait_all(plan):
    sends, arrivals = plan[:2]
    for cp, own in arrivals:
        pl.when(jnp.logical_not(own))(cp.wait_recv)
    for cp, own in sends:
        pl.when(jnp.logical_not(own))(cp.wait_send)


class Gather:
    def __init__(self, lines, full, rows, z_first):
        self.lines, self.full, self.rows, self.z_first = lines, full, rows, z_first
        self.pending = []

    def _send(self, src, peers):
        copies = [self.lines.copy(src, src, p) for p in peers]
        for cp in copies:
            cp.start()
        self.pending = copies

    def near(self):
        y, zl, c, _, zh = coords()
        mine = self.full.at[y, zl, c, pl.ds(zh * self.rows, self.rows)]
        self._send(mine, z_peers() if self.z_first else y_peers())

    def wide(self):
        self.wait()
        y, zl, c, _, zh = coords()
        if self.z_first:
            self._send(self.full.at[y, :, c], y_peers())
        else:
            self._send(self.full.at[:, zl, c, pl.ds(zh * self.rows, self.rows)], z_peers())

    def cores(self):
        self.wait()
        c = coords()[2]
        self._send(self.full.at[:, :, c], [core_peer()])

    def wait(self):
        for cp in self.pending:
            cp.wait()
        self.pending = []


def weights_kernel(qkv4, up4, down1, out1, full_q, full_u, full_d, full_o, got_q, got_u, send, recv):
    y, zl, c, x, zh = coords()
    all_weight_barrier()
    lines = Lines(send, recv)
    plan_q = spread(lines, qkv4, got_q)
    start_all(plan_q, qkv4, got_q)
    plan_u = spread(lines, up4, got_u)
    start_all(plan_u, up4, got_u)
    out_rows = full_o.at[x, zl, c, pl.ds(zh * 16, 16)]
    to_swap = lines.copy(out1, out_rows, swap_xy())
    pl.when(x != y)(to_swap.start)

    @pl.when(x == y)
    def _():
        full_o[y, zl, c, pl.ds(zh * 16, 16)] = out1[...]

    full_d[y, zl, c, pl.ds(zh * 48, 48)] = down1[...]
    g_d = Gather(lines, full_d, 48, False)
    g_d.near()
    rows = one_hot_rows(48, 64, False)
    wait_all(plan_q)
    full_q[y, zl, c, pl.ds(zh * 48, 48)] = pick(rows, got_q[...].reshape(64, got_q.shape[2]))
    g_q = Gather(lines, full_q, 48, True)
    g_q.near()
    wait_all(plan_u)
    full_u[y, zl, c, pl.ds(zh * 48, 48)] = pick(rows, got_u[...].reshape(64, got_u.shape[2]))
    g_u = Gather(lines, full_u, 48, True)
    g_u.near()
    pl.when(x != y)(to_swap.wait)
    g_o = Gather(lines, full_o, 16, False)
    g_o.near()
    order = (g_q, g_d, g_u, g_o)
    for g in order:
        g.wide()
    for g in order:
        g.cores()
    for g in order:
        g.wait()


class Scatter:
    def __init__(self, lines, part, half, near, near_in, wide, wide_in, rows, y_first):
        self.lines, self.part, self.half, self.near = lines, part, half, near
        self.near_in, self.wide, self.wide_in = near_in, wide, wide_in
        self.rows, self.y_first, self.pending = rows, y_first, []

    def wait(self):
        for cp in self.pending:
            cp.wait()
        self.pending = []

    def _start(self, copies):
        for cp in copies:
            cp.start()
        self.pending = copies

    def cores(self):
        c = coords()[2]
        self._start([self.lines.copy(self.part.at[:, :, 1 - c], self.half, core_peer())])

    def first(self):
        self.wait()
        y, zl, c, _, zh = coords()
        z, rows = zh * 2 + zl, self.rows

        @pl.loop(0, 8)
        def _(i):
            yy, zz = i // 2, i % 2
            both = self.part[yy, zz, c].astype(F32) + self.half[yy, zz].astype(F32)
            self.near[yy, zz] = both.astype(BF)

        copies = []
        for k in (1, 2, 3):
            if self.y_first:
                src, peer = self.near.at[(y + k) % 4], y_peers()[k - 1]
            else:
                zz = (z + k) % 4
                src, peer = self.near.at[:, zz % 2, pl.ds(zz // 2 * rows, rows)], z_peers()[k - 1]
            copies.append(self.lines.copy(src, self.near_in.at[k - 1], peer))
        self._start(copies)

    def second(self):
        self.wait()
        y, zl, c, _, zh = coords()
        z, rows = zh * 2 + zl, self.rows
        copies = []
        if self.y_first:
            total = self.near[y].astype(F32)
        else:
            total = self.near[:, zl, pl.ds(zh * rows, rows)].astype(F32)
        for k in range(3):
            total += self.near_in[k].astype(F32)
        self.wide[...] = total.astype(BF)
        for k in (1, 2, 3):
            if self.y_first:
                zz = (z + k) % 4
                src, peer = self.wide.at[zz % 2, pl.ds(zz // 2 * rows, rows)], z_peers()[k - 1]
            else:
                src, peer = self.wide.at[(y + k) % 4], y_peers()[k - 1]
            copies.append(self.lines.copy(src, self.wide_in.at[k - 1], peer))
        self._start(copies)

    def total(self):
        self.wait()
        y, zl, c, _, zh = coords()
        if self.y_first:
            total = self.wide[zl, pl.ds(zh * self.rows, self.rows)].astype(F32)
        else:
            total = self.wide[y].astype(F32)
        for k in range(3):
            total += self.wide_in[k].astype(F32)
        return total


def scatter_scratch(rows, n, y_first):
    half = pltpu.VMEM((4, 2, 2 * rows, n), BF)
    if y_first:
        near_in, wide = pltpu.VMEM((3, 2, 2 * rows, n), BF), pltpu.VMEM((2, 2 * rows, n), BF)
    else:
        near_in, wide = pltpu.VMEM((3, 4, rows, n), BF), pltpu.VMEM((4, rows, n), BF)
    return [half, half, near_in, wide, pltpu.VMEM((3, rows, n), BF)]


def gradients_kernel(part_q, part_u, part_d, part_o, out_q, out_u, out_d, out_o, *rest):
    send, recv = rest[-2:]
    sq, su, sd, so = rest[0:5], rest[5:10], rest[10:15], rest[15:20]
    exp_q, exp_u, fin_o = rest[20:23]
    y, zl, c, x, zh = coords()
    all_weight_barrier()
    lines = Lines(send, recv)
    todo = [
        Scatter(lines, part_d, *sd, 48, True),
        Scatter(lines, part_u, *su, 48, False),
        Scatter(lines, part_o, *so, 16, True),
        Scatter(lines, part_q, *sq, 48, False),
    ]
    for t in todo:
        t.cores()
    for t in todo:
        t.first()
    for t in todo:
        t.second()
    rows = one_hot_rows(64, 48, True)
    out_d[...] = todo[0].total().astype(BF)
    exp_u[...] = pick(rows, todo[1].total().astype(BF)).reshape(exp_u.shape)
    plan_u = gather_home(lines, exp_u, out_u)
    start_all(plan_u, exp_u, out_u)
    fin_o[...] = todo[2].total().astype(BF)
    to_swap = lines.copy(fin_o, out_o, swap_xy())
    pl.when(x != y)(to_swap.start)

    @pl.when(x == y)
    def _():
        out_o[...] = fin_o[...]

    exp_q[...] = pick(rows, todo[3].total().astype(BF)).reshape(exp_q.shape)
    plan_q = gather_home(lines, exp_q, out_q)
    start_all(plan_q, exp_q, out_q)
    wait_all(plan_u)
    pl.when(x != y)(to_swap.wait)
    wait_all(plan_q)


def call(kernel, number, ins, outs, scratch, copies):
    vmem = pl.BlockSpec(memory_space=pltpu.VMEM)
    return pl.pallas_call(
        kernel,
        out_shape=[jax.ShapeDtypeStruct(s, t) for s, t in outs],
        in_specs=[vmem] * len(ins),
        out_specs=[vmem] * len(outs),
        scratch_shapes=[*scratch, pltpu.SemaphoreType.DMA((copies,)), pltpu.SemaphoreType.DMA((copies,))],
        compiler_params=pltpu.CompilerParams(
            collective_id=number, has_side_effects=True, vmem_limit_bytes=60 * 2**20
        ),
        name=kernel.__name__,
    )(*ins)


V = pltpu.VMEM


def gather_x(a):
    (r,) = call(gather_x_kernel, 1, [a], [((4, 128, D), BF)], [], 6)
    return r.reshape(512, D)


def gather_seq(a):
    (r,) = call(gather_seq_kernel, 2, [a], [((8, 128, D), BF)], [], 13)
    return r.reshape(1024, D)


def scatter_x(parts):
    parts = parts.astype(BF).reshape(4, 128, D)
    (r,) = call(scatter_x_kernel, 3, [parts], [((128, D), F32)], [V((4, 64, D), BF), V((4, 64, D), BF)], 6)
    return r


def scatter_seq(parts):
    parts = parts.astype(BF).reshape(8, 128, D)
    quad = V((4, 64, D), BF)
    whole = V((128, D), BF)
    (r,) = call(scatter_seq_kernel, 4, [parts], [((128, D), F32)], [quad] * 4 + [whole] * 2, 13)
    return r


def normalize(values):
    r = lax.rsqrt(jnp.mean(values * values, axis=-1, keepdims=True) + EPS)
    return r, values * r


def rms_back(grad, values, r):
    return r * grad - r * r * r * values * jnp.mean(grad * values, axis=-1, keepdims=True)


def dot(a, b):
    return jnp.dot(a, b, preferred_element_type=F32)


def dot_nt(a, b):
    return lax.dot_general(a, b, (((1,), (1,)), ((), ())), preferred_element_type=F32)


def dot_tn(a, b):
    return lax.dot_general(a, b, (((0,), (0,)), ((), ())), preferred_element_type=F32)


def layout(lengths, levels):
    positions = jnp.arange(GROUP, dtype=jnp.int32)
    ends = jnp.cumsum(lengths)
    starts = ends - lengths
    ids = jnp.sum((positions[:, None] >= ends[None, :]).astype(jnp.int32), axis=1)
    one_hot = (ids[:, None] == jnp.arange(DOCS, dtype=jnp.int32)[None, :]).astype(jnp.int32)
    start = jnp.sum(one_hot * starts[None, :], axis=1)
    width = jnp.sum(one_hot * (FF // 8 * jnp.power(2, levels))[None, :], axis=1)
    return positions, start, width


def tables(offsets):
    half = HEAD_DIM // 2
    inverse = jnp.exp(jnp.arange(half, dtype=F32) * (-2.0 * math.log(10000.0) / HEAD_DIM))
    angles = offsets.astype(F32)[:, None] * inverse[None, :]
    cos, sin = jnp.cos(angles), jnp.sin(angles)
    return jnp.concatenate([cos, cos], axis=-1), jnp.concatenate([sin, sin], axis=-1)


def turn(v, cos, sin):
    v = v.reshape(v.shape[0], RANK_HEADS, HEAD_DIM)
    turned = jnp.concatenate([-v[..., 64:], v[..., :64]], axis=-1)
    return (v * cos[:, None, :] + turned * sin[:, None, :]).reshape(v.shape[0], RANK_COLS)


def turn_back(v, cos, sin):
    v = v.reshape(v.shape[0], RANK_HEADS, HEAD_DIM)
    w = v * sin[:, None, :]
    turned = jnp.concatenate([w[..., 64:], -w[..., :64]], axis=-1)
    return (v * cos[:, None, :] + turned).reshape(v.shape[0], RANK_COLS)


def heads(v):
    return v.reshape(v.shape[0], RANK_HEADS, HEAD_DIM).transpose(1, 0, 2)


def unheads(v):
    return v.transpose(1, 0, 2).reshape(v.shape[1], RANK_COLS)


def bmm(spec, a, b):
    return jnp.einsum(spec, a, b, preferred_element_type=F32)


def per_device(
    block_input, doc_lengths, ffn_levels, attn_gain, qkv_weight, out_weight, ffn_gain, up_weight, down_weight, grad_output
):
    _, _, _, x, zh = coords()
    scale = HEAD_DIM**-0.5
    gain_one = attn_gain.astype(F32)[:, None]
    gain_two = ffn_gain.astype(F32)[:, None]
    w_qkv = (qkv_weight.astype(F32) * gain_one).astype(BF)
    w_up = (up_weight.astype(F32) * gain_two).astype(BF)
    pad = ((0, 0), (0, 4), (0, 0))
    qkv4 = jnp.pad(w_qkv.reshape(12, 3, 4, RANK_COLS).transpose(2, 0, 1, 3).reshape(4, 12, 1152), pad)
    up4 = jnp.pad(w_up.reshape(12, 16, 4, 96).transpose(2, 0, 1, 3).reshape(4, 12, D), pad)
    out1 = jnp.pad(out_weight, ((0, 4), (0, 0)))
    full_q, full_u, full_d, full_o = call(
        weights_kernel, 5, [qkv4, up4, down_weight, out1],
        [((4, 2, 2, 96, 1152), BF), ((4, 2, 2, 96, D), BF), ((4, 2, 2, 96, D), BF), ((4, 2, 2, 32, D), BF)],
        [V((4, 16, 1152), BF), V((4, 16, D), BF)], 40,
    )
    wq, wk, wv = jnp.split(full_q.reshape(D, 1152), 3, axis=1)
    wu, wd = full_u.reshape(D, D), full_d.reshape(D, D)
    wo = full_o.reshape(4, 2, 2, 2, 16, D)[:, :, :, :, :12].transpose(1, 2, 0, 3, 4, 5).reshape(RANK_COLS, D)

    positions, start, width = layout(doc_lengths[0], ffn_levels[0])
    mine = lambda v: lax.dynamic_index_in_dim(v.reshape(4, 2, 128, *v.shape[1:]), zh, 1, False).reshape(512, *v.shape[1:])
    cos, sin = tables(positions - start)
    cos_q, sin_q = mine(cos), mine(sin)
    pos_q, start_q, width_q = mine(positions), mine(start), mine(width)
    allowed = (positions[None, :] <= pos_q[:, None]) & (positions[None, :] >= start_q[:, None])
    col = jnp.arange(D, dtype=jnp.int32)
    unit = col // 96 * 384 + x * 96 + col % 96
    unit_mask = (unit[None, :] < width_q[:, None]).astype(F32)

    inputs = block_input[0].astype(F32)
    r_one, hat_one = normalize(inputs)
    normed = gather_seq(hat_one.astype(BF))
    normed_q = mine(normed)
    q = heads(turn(dot(normed_q, wq), cos_q, sin_q).astype(BF))
    k = heads(turn(dot(normed, wk), cos, sin).astype(BF))
    v = heads(dot(normed, wv).astype(BF))
    scores = jnp.where(allowed[None], bmm("hqd,hkd->hqk", q, k) * scale, -1e30)
    probs = jax.nn.softmax(scores, axis=-1)
    rounded = probs.astype(BF)
    attended = unheads(bmm("hqk,hkd->hqd", rounded, v)).astype(BF)
    middle = inputs + scatter_x(dot(attended, wo))
    r_two, hat_two = normalize(middle)
    normed_two = gather_x(hat_two.astype(BF))
    pre = dot(normed_two, wu)
    act, gelu_back = jax.vjp(jax.nn.gelu, pre)
    hidden = (act * unit_mask).astype(BF)
    block_output = middle + scatter_x(dot(hidden, wd))

    up_grad = gather_x(grad_output[0])
    pre_grad = gelu_back(dot_nt(up_grad, wd) * unit_mask)[0].astype(BF)
    d_down = dot_tn(hidden, up_grad)
    d_up = dot_tn(normed_two, pre_grad)
    h_two = scatter_x(dot_nt(pre_grad, wu))
    middle_grad = grad_output[0].astype(F32) + rms_back(h_two, middle, r_two)
    branch = gather_x(middle_grad.astype(BF))
    d_out = dot_tn(attended, branch)
    att_grad = heads(dot_nt(branch, wo).astype(BF))
    prob_grad = bmm("hqd,hkd->hqk", att_grad, v)
    score_grad = (probs * (prob_grad - jnp.sum(probs * prob_grad, axis=-1, keepdims=True))).astype(BF)
    dq = unheads(bmm("hqk,hkd->hqd", score_grad, k)) * scale
    dk = unheads(bmm("hqk,hqd->hkd", score_grad, q)) * scale
    dv = unheads(bmm("hqk,hqd->hkd", rounded, att_grad)).astype(BF)
    dq = turn_back(dq, cos_q, sin_q).astype(BF)
    dk = turn_back(dk, cos, sin).astype(BF)
    d_qkv = jnp.concatenate([dot_tn(normed_q, dq), dot_tn(normed, dk), dot_tn(normed, dv)], axis=1)
    first = (dot_nt(dk, wk) + dot_nt(dv, wv)).reshape(4, 2, 128, D)
    first_q = dot_nt(dq, wq).reshape(4, 128, D)
    first += jnp.where((jnp.arange(2) == zh)[None, :, None, None], first_q[:, None], 0.0)
    h_one = scatter_seq(first)
    grad_input = middle_grad + rms_back(h_one, inputs, r_one)

    d_out = d_out.reshape(2, 2, 4, 2, 12, D).transpose(2, 0, 1, 3, 4, 5)
    d_out = jnp.pad(d_out, ((0, 0),) * 4 + ((0, 4), (0, 0))).reshape(4, 2, 2, 32, D)
    part_shape = lambda n: (4, 2, 2, 96, n)
    got_q, got_u, got_d, got_o = call(
        gradients_kernel, 6,
        [d_qkv.astype(BF).reshape(part_shape(1152)), d_up.astype(BF).reshape(part_shape(D)),
         d_down.astype(BF).reshape(part_shape(D)), d_out.astype(BF)],
        [((4, 16, 1152), BF), ((4, 16, D), BF), ((48, D), BF), ((16, D), BF)],
        scatter_scratch(48, 1152, False) + scatter_scratch(48, D, False) + scatter_scratch(48, D, True)
        + scatter_scratch(16, D, True) + [V((4, 16, 1152), BF), V((4, 16, D), BF), V((16, D), BF)], 48,
    )
    raw_qkv = got_q[:, :12].reshape(4, 12, 3, RANK_COLS).transpose(1, 2, 0, 3).reshape(12, 4608).astype(F32)
    raw_up = got_u[:, :12].reshape(4, 12, 16, 96).transpose(1, 2, 0, 3).reshape(12, FF).astype(F32)
    grad_attn_gain = jnp.sum(raw_qkv * qkv_weight.astype(F32), axis=1)
    grad_ffn_gain = jnp.sum(raw_up * up_weight.astype(F32), axis=1)
    return (
        block_output.astype(BF)[None],
        grad_input[None],
        grad_attn_gain,
        raw_qkv * gain_one,
        got_o[:12].astype(F32),
        grad_ffn_gain,
        raw_up * gain_two,
        got_d.astype(F32),
    )


def solution(mesh):
    rows = P("batch", "seq", None)
    every = ("batch", "seq")
    return jax.shard_map(
        per_device,
        mesh=mesh,
        in_specs=(rows, P("batch", None), P("batch", None), P(every), P(every, None), P(every, None), P(every),
                  P(every, None), P(every, None), rows),
        out_specs=(rows, rows, P(every), P(every, None), P(every, None), P(every), P(every, None), P(every, None)),
        check_vma=False,
    )
```

```python
import math

import jax
import jax.numpy as jnp
import numpy as np
from jax import lax
from jax.experimental import pallas as pl
from jax.experimental.pallas import tpu as pltpu
from jax.sharding import PartitionSpec as P

HEADS = 12
HEAD_DIM = 128
D = 1536
FF = 6144
DOCS = 6
GROUP = 1024
SHARD = 128
RANK_HEADS = 3
RANK_COLS = 384
EPS = 1e-06
VMEM_LIMIT = 63 * 2**20
BF = jnp.bfloat16
F32 = jnp.float32
MESH = pl.DeviceIdType.MESH


def coords():
    b = lax.axis_index("batch")
    s = lax.axis_index("seq")
    return b // 4, (b // 2) % 2, b % 2, s // 2, s % 2


def dev(y, zl, c, x, zh):
    return (y * 4 + zl * 2 + c, x * 2 + zh)


def x_peers():
    y, zl, c, x, zh = coords()
    return [dev(y, zl, c, (x + k) % 4, zh) for k in (1, 2, 3)]


def y_peers():
    y, zl, c, x, zh = coords()
    return [dev((y + k) % 4, zl, c, x, zh) for k in (1, 2, 3)]


def z_peers():
    y, zl, c, x, zh = coords()
    z = zh * 2 + zl
    return [dev(y, (z + k) % 2, c, x, ((z + k) % 4) // 2) for k in (1, 2, 3)]


def core_peer():
    y, zl, c, x, zh = coords()
    return dev(y, zl, 1 - c, x, zh)


def zh_peer():
    y, zl, c, x, zh = coords()
    return dev(y, zl, c, x, 1 - zh)


class Lines:
    def __init__(self, send, recv):
        self.send, self.recv, self.used = send, recv, 0

    def copy(self, src, dst, peer):
        at = self.used
        self.used += 1
        return pltpu.make_async_remote_copy(
            src, dst, self.send.at[at], self.recv.at[at], device_id=peer, device_id_type=MESH
        )


LO, HI = pl.ds(0, 64), pl.ds(64, 64)


class RingGather:
    def __init__(self, lines, slot):
        self.lines, self.slot = lines, slot

    def start(self):
        x = coords()[3]
        nxt, _, prv = x_peers()
        lo, hi = self.slot(x).at[LO], self.slot(x).at[HI]
        self.first = self.lines.copy(lo, lo, nxt)
        self.second = self.lines.copy(hi, hi, prv)
        self.rest = [self.lines.copy(hi, hi, nxt), self.lines.copy(lo, lo, prv)]
        for cp in (self.first, self.second, *self.rest):
            cp.start()

    def on(self):
        x = coords()[3]
        nxt, _, prv = x_peers()
        lo, hi = self.slot((x + 3) % 4).at[LO], self.slot((x + 1) % 4).at[HI]
        self.first.wait_recv()
        one = self.lines.copy(lo, lo, nxt)
        one.start()
        self.second.wait_recv()
        two = self.lines.copy(hi, hi, prv)
        two.start()
        self.rest += [one, two]

    def finish(self):
        self.first.wait_send()
        self.second.wait_send()
        for cp in self.rest:
            cp.wait()


class RingScatter:
    def __init__(self, lines, part, got, via):
        self.lines, self.part, self.got, self.via = lines, part, got, via

    def start(self):
        x = coords()[3]
        nxt, _, prv = x_peers()
        left, right, far = (x + 3) % 4, (x + 1) % 4, (x + 2) % 4
        part = self.part
        self.far_lo = self.lines.copy(part(far).at[LO], self.via.at[0], nxt)
        self.far_hi = self.lines.copy(part(far).at[HI], self.via.at[1], prv)
        self.rest = [
            self.lines.copy(part(right).at[HI], self.got.at[2], nxt),
            self.lines.copy(part(left).at[LO], self.got.at[0], prv),
        ]
        for cp in (self.far_lo, self.far_hi, *self.rest):
            cp.start()

    def on(self):
        x = coords()[3]
        nxt, _, prv = x_peers()
        left, right = (x + 3) % 4, (x + 1) % 4
        via = self.via
        self.far_lo.wait_recv()
        via[0] = (via[0].astype(F32) + self.part(right)[LO].astype(F32)).astype(BF)
        one = self.lines.copy(via.at[0], self.got.at[1], nxt)
        one.start()
        self.far_hi.wait_recv()
        via[1] = (via[1].astype(F32) + self.part(left)[HI].astype(F32)).astype(BF)
        two = self.lines.copy(via.at[1], self.got.at[3], prv)
        two.start()
        self.rest += [one, two]

    def finish(self):
        self.far_lo.wait_send()
        self.far_hi.wait_send()
        for cp in self.rest:
            cp.wait()

    def total(self, own):
        got = self.got
        lo = got[0].astype(F32) + got[1].astype(F32)
        hi = got[2].astype(F32) + got[3].astype(F32)
        return own + jnp.concatenate([lo, hi], axis=0)


def one_hot_rows(rows, cols, expand):
    i = lax.broadcasted_iota(jnp.int32, (rows, cols), 0)
    j = lax.broadcasted_iota(jnp.int32, (rows, cols), 1)
    a, p = (j, i) if expand else (i, j)
    return jnp.where((p % 16 < 12) & (p // 16 * 12 + p % 16 == a), 1.0, 0.0).astype(BF)


def pick(matrix, values):
    return jnp.dot(matrix, values, preferred_element_type=F32).astype(BF)


def seq_peers():
    y, zl, c, x, zh = coords()
    s = x * 2 + zh
    found = []
    for k in range(1, 8):
        t = (s + k) % 8
        found.append(dev(y, zl, c, t // 2, t % 2))
    return found


def greet():
    y, _, _, x, _ = coords()
    sem = pltpu.get_barrier_semaphore()
    peers = seq_peers() + y_peers() + z_peers()[::2] + [core_peer()]
    for peer in peers:
        pl.semaphore_signal(sem, inc=1, device_id=peer, device_id_type=MESH)

    @pl.when(x != y)
    def _():
        pl.semaphore_signal(sem, inc=1, device_id=swap_xy(), device_id_type=MESH)

    return len(peers) + jnp.where(x != y, 1, 0)


def swap_xy():
    y, zl, c, x, zh = coords()
    return dev(x, zl, c, y, zh)


def spread(lines, src, dst):
    y, zl, c, x, zh = coords()
    s = x * 2 + zh
    at = lines.used
    lines.used += 4
    sends, arrivals = [], []
    for k in range(4):
        i = (x + k) % 4
        own = (i == x) & (x // 2 == zh)
        cp = pltpu.make_async_remote_copy(
            src.at[i], dst.at[s % 4], lines.send.at[at + k], lines.recv.at[at + s % 4],
            device_id=dev(y, zl, c, i, x // 2), device_id_type=MESH,
        )
        sends.append((cp, own))
    for j in range(4):
        own = (x // 2 == zh) & (s % 4 == j)
        cp = pltpu.make_async_remote_copy(
            src.at[j], dst.at[j], lines.send.at[at], lines.recv.at[at + j],
            device_id=core_peer(), device_id_type=MESH,
        )
        arrivals.append((cp, own))
    return sends, arrivals, (x // 2 == zh), x, s % 4


def gather_home(lines, src, dst):
    y, zl, c, x, zh = coords()
    s = x * 2 + zh
    at = lines.used
    lines.used += 4
    sends, arrivals = [], []
    for k in range(4):
        i = (s + k) % 4
        t = 4 * zh + i
        own = t == s
        cp = pltpu.make_async_remote_copy(
            src.at[i], dst.at[x], lines.send.at[at + k], lines.recv.at[at + x],
            device_id=dev(y, zl, c, t // 2, t % 2), device_id_type=MESH,
        )
        sends.append((cp, own))
    for j in range(4):
        own = (x // 2 == zh) & (x == j)
        cp = pltpu.make_async_remote_copy(
            src.at[j], dst.at[j], lines.send.at[at], lines.recv.at[at + j],
            device_id=core_peer(), device_id_type=MESH,
        )
        arrivals.append((cp, own))
    return sends, arrivals, (x // 2 == zh), s % 4, x


def start_all(plan, src, dst):
    sends, _, mine, from_slot, to_slot = plan
    for cp, own in sends:
        pl.when(jnp.logical_not(own))(cp.start)

    @pl.when(mine)
    def _():
        dst[to_slot] = src[from_slot]


def wait_all(plan):
    sends, arrivals = plan[:2]
    for cp, own in arrivals:
        pl.when(jnp.logical_not(own))(cp.wait_recv)
    for cp, own in sends:
        pl.when(jnp.logical_not(own))(cp.wait_send)


class Gather:
    def __init__(self, lines, full, rows, z_first, y_inner=False, columns=None):
        self.lines, self.full, self.rows, self.z_first, self.y_inner = lines, full, rows, z_first, y_inner
        self.columns = pl.ds(0, full.shape[-1]) if columns is None else columns
        self.pending = []

    def _at(self, y, zl, c, rows):
        place = (zl, c, y) if self.y_inner else (y, zl, c)
        return self.full.at[(*place, rows, self.columns)]

    def _send(self, src, peers):
        copies = [self.lines.copy(src, src, p) for p in peers]
        for cp in copies:
            cp.start()
        self.pending = copies

    def near(self):
        y, zl, c, _, zh = coords()
        mine = self._at(y, zl, c, pl.ds(zh * self.rows, self.rows))
        self._send(mine, z_peers() if self.z_first else y_peers())

    def wide(self):
        self.wait()
        y, zl, c, _, zh = coords()
        if self.z_first:
            self._send(self._at(y, slice(None), c, pl.ds(0, 2 * self.rows)), y_peers())
        else:
            self._send(self._at(slice(None), zl, c, pl.ds(zh * self.rows, self.rows)), z_peers())

    def cores(self):
        self.wait()
        c = coords()[2]
        self._send(self._at(slice(None), slice(None), c, pl.ds(0, 2 * self.rows)), [core_peer()])

    def wait(self):
        for cp in self.pending:
            cp.wait()
        self.pending = []


class Scatter:
    def __init__(self, lines, part, bufs, rows, y_first, y_inner=False, columns=None):
        self.lines, self.part = lines, part
        self.half, self.near_in, self.wide, self.wide_in = bufs
        self.rows, self.y_first, self.y_inner, self.pending = rows, y_first, y_inner, []
        self.columns = pl.ds(0, part.shape[-1]) if columns is None else columns

    def wait(self):
        for cp in self.pending:
            cp.wait()
        self.pending = []

    def _start(self, copies):
        for cp in copies:
            cp.start()
        self.pending = copies

    def cores(self):
        c = coords()[2]
        rows = pl.ds(0, 2 * self.rows)
        place = (slice(None), 1 - c, slice(None)) if self.y_inner else (slice(None), slice(None), 1 - c)
        self._start([self.lines.copy(self.part.at[(*place, rows, self.columns)], self.half, core_peer())])

    def first(self):
        self.wait()
        y, zl, c, _, zh = coords()
        z, rows, inner = zh * 2 + zl, self.rows, self.half.shape[1]

        @pl.loop(0, 8)
        def _(i):
            a, b = i // inner, i % inner
            place = (a, c, b) if self.y_inner else (a, b, c)
            both = self.part[(*place, slice(None), self.columns)].astype(F32) + self.half[a, b].astype(F32)
            self.half[a, b] = both.astype(BF)

        copies = []
        for k in (1, 2, 3):
            if self.y_first:
                yy = (y + k) % 4
                src, peer = self.half.at[:, yy] if self.y_inner else self.half.at[yy], y_peers()[k - 1]
            else:
                zz = (z + k) % 4
                src, peer = self.half.at[:, zz % 2, pl.ds(zz // 2 * rows, rows)], z_peers()[k - 1]
            copies.append(self.lines.copy(src, self.near_in.at[k - 1], peer))
        self._start(copies)

    def second(self):
        self.wait()
        y, zl, c, _, zh = coords()
        z, rows = zh * 2 + zl, self.rows
        copies = []
        for i in range(self.wide.shape[0]):
            if self.y_first:
                total = (self.half[i, y] if self.y_inner else self.half[y, i]).astype(F32)
            else:
                total = self.half[i, zl, pl.ds(zh * rows, rows)].astype(F32)
            for k in range(3):
                total += self.near_in[k, i].astype(F32)
            self.wide[i] = total.astype(BF)
        for k in (1, 2, 3):
            if self.y_first:
                zz = (z + k) % 4
                src, peer = self.wide.at[zz % 2, pl.ds(zz // 2 * rows, rows)], z_peers()[k - 1]
            else:
                src, peer = self.wide.at[(y + k) % 4], y_peers()[k - 1]
            copies.append(self.lines.copy(src, self.wide_in.at[k - 1], peer))
        self._start(copies)

    def total(self):
        self.wait()
        y, zl, c, _, zh = coords()
        if self.y_first:
            total = self.wide[zl, pl.ds(zh * self.rows, self.rows)].astype(F32)
        else:
            total = self.wide[y].astype(F32)
        for k in range(3):
            total += self.wide_in[k].astype(F32)
        return total


def scatter_scratch(rows, n, y_first, y_inner=False):
    half = pltpu.VMEM((2, 4, 2 * rows, n) if y_inner else (4, 2, 2 * rows, n), BF)
    if y_first:
        near_in, wide = pltpu.VMEM((3, 2, 2 * rows, n), BF), pltpu.VMEM((2, 2 * rows, n), BF)
    else:
        near_in, wide = pltpu.VMEM((3, 4, rows, n), BF), pltpu.VMEM((4, rows, n), BF)
    return [half, near_in, wide, pltpu.VMEM((3, rows, n), BF)]


def dot(a, b):
    return jnp.dot(a, b, preferred_element_type=F32)


def dot_nt(a, b):
    return lax.dot_general(a, b, (((1,), (1,)), ((), ())), preferred_element_type=F32)


def dot_tn(a, b):
    return lax.dot_general(a, b, (((0,), (0,)), ((), ())), preferred_element_type=F32)


def normalize(values):
    r = lax.rsqrt(jnp.mean(values * values, axis=-1, keepdims=True) + EPS)
    return r, values * r


def rms_back(grad, values):
    r, hat = normalize(values)
    return r * (grad - hat * jnp.mean(grad * hat, axis=-1, keepdims=True))


def cos_sin(table):
    other = pltpu.roll(table, 64, 1)
    low = lax.broadcasted_iota(jnp.int32, table.shape, 1) < 64
    return jnp.where(low, table, other), jnp.where(low, -other, table)


def turn(v, cos, sin):
    return v * cos + pltpu.roll(v, 64, 1) * sin


def turn_back(v, cos, sin):
    return v * cos - pltpu.roll(v, 64, 1) * sin


GELU_A, GELU_B = math.sqrt(2.0 / math.pi), 0.044715


def gelu_both(v):
    square = v * v
    t = jnp.tanh(GELU_A * v * (1.0 + GELU_B * square))
    half = 0.5 * (1.0 + t)
    return v * half, half + 0.5 * v * (1.0 - t * t) * (GELU_A * (1.0 + 3.0 * GELU_B * square))


def cols(i, n):
    return pl.ds(pl.multiple_of(i * n, n), n)


NAMES = (
    "full_q", "full_u", "full_d", "full_o", "got_q", "got_u", "src_q", "src_u", "src_o",
    "normed", "q_ref", "k_ref", "v_ref", "p0", "p1", "p2", "p3",
    "att", "att_grad", "middle", "wo", "ntwo", "up_grad", "hidden", "pre_grad", "branch", "part_a", "part_c",
    "got_a", "via_a", "got_b", "via_b", "got_c", "via_c", "swap_out", "swap_in", "dk_t", "dv_t",
    "sq0", "sq1", "sq2", "sq3", "sr0", "sr1", "sr2", "sr3", "su0", "su1", "su2", "su3",
    "sd0", "sd1", "sd2", "sd3", "so0", "so1", "so2", "so3", "fin_o", "fin_d", "send", "recv",
)


def scratch_list():
    V = pltpu.VMEM
    block = V((4, 128, D), BF)
    got, via = V((4, 64, D), BF), V((2, 64, D), BF)
    kv = V((3, 4, 2, 128, 128), BF)
    shapes = [V((4, 2, 2, 96, 1152), BF), V((4, 2, 2, 96, D), BF), V((2, 2, 4, 96, D), BF), V((2, 2, 4, 32, D), BF)]
    shapes += [V((4, 16, 1152), BF), V((4, 16, D), BF)] * 2 + [V((16, D), BF)]
    shapes += [V((4, 2, 128, D), BF), V((3, 4, 128, 128), BF), kv, kv]
    shapes += [V((3, 128, 256 * (i + 1)), BF) for i in range(4)]
    shapes += [V((4, 128, RANK_COLS), BF), V((4, 128, RANK_COLS), BF), V((128, D), F32), V((RANK_COLS, D), BF)]
    shapes += [block] * 7
    shapes += [got, via] * 3 + [V((128, D), BF), V((128, D), BF)]
    shapes += [V((128, GROUP), F32), V((128, GROUP), F32)]
    shapes += scatter_scratch(48, 640, False) + scatter_scratch(48, 512, True) + scatter_scratch(48, D, False)
    shapes += scatter_scratch(48, D, True, True) + scatter_scratch(16, D, True, True)
    shapes += [V((16, D), BF), V((48, D), BF)]
    shapes += [pltpu.SemaphoreType.DMA((160,)), pltpu.SemaphoreType.DMA((160,))]
    assert len(shapes) == len(NAMES)
    return shapes


class Refs:
    pass


def column(row):
    n = row.shape[1]
    same = lax.broadcasted_iota(jnp.int32, (n, n), 0) == lax.broadcasted_iota(jnp.int32, (n, n), 1)
    return jnp.sum(jnp.where(same, row, 0.0), axis=1, keepdims=True)


def as_row(col):
    n = col.shape[0]
    same = lax.broadcasted_iota(jnp.int32, (n, n), 0) == lax.broadcasted_iota(jnp.int32, (n, n), 1)
    return jnp.sum(jnp.where(same, col, 0.0), axis=0, keepdims=True)


def sixteen(rows):
    return jnp.concatenate([rows, jnp.zeros((4, rows.shape[1]), rows.dtype)], axis=0).astype(BF)


def documents(lengths, levels, positions):
    start, width = jnp.zeros_like(positions), jnp.zeros_like(positions)
    first = 0
    for d in range(DOCS):
        level = levels[0, d]
        wide = jnp.where(level == 0, FF // 8, jnp.where(level == 1, FF // 4, jnp.where(level == 2, FF // 2, FF)))
        inside = positions >= first
        start = jnp.where(inside, first, start)
        width = jnp.where(inside, wide, width)
        first = first + lengths[0, d]
    return start, width


def layer_kernel(
    lengths, levels, tokens, grad_in, qkv, out_w, up, down, gain_one, gain_two, angles,
    block_out, grad_input, out_q, out_u, out_d, out_o, *scratch
):
    g = Refs()
    for name, ref in zip(NAMES, scratch):
        setattr(g, name, ref)
    y, zl, c, x, zh = coords()
    lines = Lines(g.send, g.recv)
    scale = HEAD_DIM**-0.5
    greetings = greet()

    g.normed[x, zh] = normalize(tokens[...].astype(F32))[1].astype(BF)
    g.up_grad[x] = grad_in[...]
    one, two = column(gain_one[...].astype(F32)), column(gain_two[...].astype(F32))
    for i in range(4):
        for j in range(3):
            at = j * D + i * RANK_COLS
            g.src_q[i, :, j * RANK_COLS : (j + 1) * RANK_COLS] = sixteen(qkv[:, at : at + RANK_COLS].astype(F32) * one)
        g.src_u[i] = sixteen(up[:, i * D : (i + 1) * D].astype(F32) * two)
    g.src_o[...] = sixteen(out_w[...].astype(F32))
    pl.semaphore_wait(pltpu.get_barrier_semaphore(), greetings)

    ring_one = RingGather(lines, lambda i: g.normed.at[i, zh])
    ring_two = RingGather(lines, lambda i: g.normed.at[i, 1 - zh])
    swap = lines.copy(g.normed.at[x, zh], g.normed.at[x, zh], zh_peer())
    plan_q = spread(lines, g.src_q, g.got_q)
    start_all(plan_q, g.src_q, g.got_q)
    ring_one.start()
    swap.start()
    plan_u = spread(lines, g.src_u, g.got_u)
    start_all(plan_u, g.src_u, g.got_u)
    swap_o = lines.copy(g.src_o, g.full_o.at[zl, c, x, pl.ds(zh * 16, 16)], swap_xy())
    swap_d = lines.copy(down, g.full_d.at[zl, c, x, pl.ds(zh * 48, 48)], swap_xy())

    @pl.when(x != y)
    def _():
        swap_o.start()
        swap_d.start()

    @pl.when(x == y)
    def _():
        g.full_o[zl, c, x, pl.ds(zh * 16, 16)] = g.src_o[...]
        g.full_d[zl, c, x, pl.ds(zh * 48, 48)] = down[...]

    rows = one_hot_rows(48, 64, False)
    wait_all(plan_q)
    g.full_q[y, zl, c, pl.ds(zh * 48, 48)] = pick(rows, g.got_q[...].reshape(64, 1152))
    gather_q = [
        Gather(lines, g.full_q, 48, True, False, pl.ds(0, 640)),
        Gather(lines, g.full_q, 48, False, False, pl.ds(640, 512)),
    ]
    for t in gather_q:
        t.near()
    ring_one.on()
    for t in gather_q:
        t.wide()
    gather_o = Gather(lines, g.full_o, 16, False, True)
    gather_u = Gather(lines, g.full_u, 48, True)
    gather_d = Gather(lines, g.full_d, 48, False, True)

    @pl.when(x != y)
    def _():
        swap_o.wait()
        swap_d.wait()

    gather_o.near()
    swap.wait_recv()
    ring_two.start()
    wait_all(plan_u)
    g.full_u[y, zl, c, pl.ds(zh * 48, 48)] = pick(rows, g.got_u[...].reshape(64, D))
    gather_d.near()
    gather_u.near()
    ring_one.finish()
    for t in gather_q:
        t.cores()
    gather_o.wide()
    ring_two.on()
    for t in gather_q:
        t.wait()

    def project(zz, own_half):
        block = g.normed[:, zz].reshape(512, D)
        cos_b, sin_b = cos_sin(angles[:, zz].reshape(512, 128))
        for j in range(0 if own_half else 1, 3):
            made = dot(block, g.full_q[:, :, :, :, j * RANK_COLS : (j + 1) * RANK_COLS].reshape(D, RANK_COLS))
            for h in range(RANK_HEADS):
                head = made[:, h * 128 : (h + 1) * 128]
                if j < 2:
                    head = turn(head, cos_b, sin_b)
                head = head.astype(BF).reshape(4, 128, 128)
                if j == 0:
                    g.q_ref[h] = head
                elif j == 1:
                    g.k_ref[h, :, zz] = head
                else:
                    g.v_ref[h, :, zz] = head

    project(zh, True)
    ring_two.finish()
    swap.wait_send()
    ring_up = RingGather(lines, lambda i: g.up_grad.at[i])
    ring_up.start()
    gather_d.wide()
    gather_u.wide()
    project(1 - zh, False)
    gather_o.cores()

    probs = [g.p0, g.p1, g.p2, g.p3]

    @pl.loop(0, RANK_HEADS)
    def _(h):
        for i in range(4):
            n = 256 * (i + 1)
            keys = g.k_ref[h, : i + 1].reshape(n, 128)
            values = g.v_ref[h, : i + 1].reshape(n, 128)
            scores = dot_nt(g.q_ref[h, i], keys) * scale
            base = (2 * i + zh) * 128
            q_at = base + lax.broadcasted_iota(jnp.int32, (128, n), 0)
            k_at = lax.broadcasted_iota(jnp.int32, (128, n), 1)
            first = documents(lengths, levels, base + lax.broadcasted_iota(jnp.int32, (128, 1), 0))[0]
            scores = jnp.where((k_at <= q_at) & (k_at >= first), scores, -1e30)
            e = jnp.exp(scores - jnp.max(scores, axis=-1, keepdims=True))
            p = (e * (1.0 / jnp.sum(e, axis=-1, keepdims=True))).astype(BF)
            probs[i][h] = p
            g.att[i, :, pl.ds(pl.multiple_of(h * 128, 128), 128)] = dot(p, values).astype(BF)

    ring_up.on()
    gather_o.wait()
    g.wo[...] = pick(one_hot_rows(RANK_COLS, 512, False), g.full_o[...].reshape(512, D))

    def to_parts(parts, left, right_of, transposed, tiles):
        n = D // tiles

        @pl.loop(0, tiles)
        def _(t):
            right = right_of(t)
            made = dot_nt(left, right) if transposed else dot(left, right)
            parts[:, :, cols(t, n)] = made.astype(BF).reshape(4, 128, n)

    to_parts(g.part_a, g.att[...].reshape(512, RANK_COLS), lambda t: g.wo[:, cols(t, 512)], False, 3)
    ring_a = RingScatter(lines, lambda i: g.part_a.at[i], g.got_a, g.via_a)
    ring_a.start()
    ring_up.finish()
    ring_a.on()
    ring_a.finish()
    g.middle[...] = ring_a.total(tokens[...].astype(F32) + g.part_a[x].astype(F32))
    g.ntwo[x] = normalize(g.middle[...])[1].astype(BF)
    ring_n = RingGather(lines, lambda i: g.ntwo.at[i])
    ring_n.start()
    gather_d.cores()
    gather_u.cores()
    ring_n.on()

    def full_rows(ref, t):
        return ref[pl.ds(t * 2, 2)].reshape(768, ref.shape[-1])

    def full_cols(ref, t, n):
        return ref[:, :, :, :, cols(t, n)].reshape(D, n)

    gather_d.wait()
    up_all = g.up_grad[...].reshape(512, D)
    to_parts(g.pre_grad, up_all, lambda t: g.full_d[t].reshape(768, D), True, 2)
    gather_u.wait()
    ring_n.finish()

    width = jnp.concatenate(
        [
            documents(lengths, levels, (2 * i + zh) * 128 + lax.broadcasted_iota(jnp.int32, (128, 1), 0))[1]
            for i in range(4)
        ],
        axis=0,
    )

    @pl.loop(0, 6)
    def _(t):
        pre = dot(g.ntwo[...].reshape(512, D), full_cols(g.full_u, t, 256))
        unit = x * D + t * 256 + lax.broadcasted_iota(jnp.int32, (512, 256), 1)
        mask = unit < width
        act, slope = gelu_both(pre)
        g.hidden[:, :, cols(t, 256)] = jnp.where(mask, act, 0.0).astype(BF).reshape(4, 128, 256)
        back = g.pre_grad[:, :, cols(t, 256)].reshape(512, 256).astype(F32)
        g.pre_grad[:, :, cols(t, 256)] = jnp.where(mask, slope * back, 0.0).astype(BF).reshape(4, 128, 256)

    pre_all = g.pre_grad[...].reshape(512, D)
    to_parts(g.part_a, pre_all, lambda t: full_rows(g.full_u, t), True, 2)
    ring_b = RingScatter(lines, lambda i: g.part_a.at[i], g.got_b, g.via_b)
    ring_b.start()

    def weight_grad(full, left_of, right):
        @pl.loop(0, 4)
        def _(t):
            made = dot_tn(left_of(t), right).astype(BF)
            if full.shape[0] == 4:
                full[t] = made.reshape(full.shape[1:])
            else:
                full[t // 2, t % 2] = made.reshape(full.shape[2:])

    weight_grad(g.full_u, lambda t: g.ntwo[:, :, cols(t, 384)].reshape(512, 384), pre_all)
    scatter_u = Scatter(lines, g.full_u, (g.su0, g.su1, g.su2, g.su3), 48, False)
    scatter_u.cores()
    ring_b.on()
    to_parts(g.part_c, g.hidden[...].reshape(512, D), lambda t: full_cols(g.full_d, t, 512), False, 3)
    scatter_u.first()
    weight_grad(g.full_d, lambda t: g.hidden[:, :, cols(t, 384)].reshape(512, 384), up_all)
    scatter_d = Scatter(lines, g.full_d, (g.sd0, g.sd1, g.sd2, g.sd3), 48, True, True)
    scatter_d.cores()
    ring_b.finish()

    grad_input[...] = grad_in[...].astype(F32) + rms_back(ring_b.total(g.part_a[x].astype(F32)), g.middle[...])
    g.branch[x] = grad_input[...].astype(BF)
    ring_g = RingGather(lines, lambda i: g.branch.at[i])
    ring_g.start()
    scatter_d.first()
    ring_g.on()
    ring_g.finish()
    ring_c = RingScatter(lines, lambda i: g.part_c.at[i], g.got_c, g.via_c)
    ring_c.start()

    branch_all = g.branch[...].reshape(512, D)
    g.att_grad[...] = dot_nt(branch_all, g.wo[...]).astype(BF).reshape(4, 128, RANK_COLS)

    @pl.loop(0, RANK_HEADS)
    def _(h):
        at = pl.ds(pl.multiple_of(h * 128, 128), 128)
        g.dk_t[...] = jnp.zeros_like(g.dk_t)
        g.dv_t[...] = jnp.zeros_like(g.dv_t)
        for i in range(4):
            n = 256 * (i + 1)
            keys = g.k_ref[h, : i + 1].reshape(n, 128)
            values = g.v_ref[h, : i + 1].reshape(n, 128)
            queries = g.q_ref[h, i]
            p = probs[i][h]
            grad = g.att_grad[i, :, at]
            delta = jnp.sum(grad.astype(F32) * g.att[i, :, at].astype(F32), axis=-1, keepdims=True)
            ds = (p.astype(F32) * (dot_nt(grad, values) - delta)).astype(BF)
            dq = dot(ds, keys) * scale
            g.dk_t[:, :n] += dot(queries.T, ds)
            g.dv_t[:, :n] += dot(grad.T, p)
            g.q_ref[h, i] = turn_back(dq, *cos_sin(angles[i, zh])).astype(BF)
        dk = g.dk_t[...].T * scale
        dk = turn_back(dk, *cos_sin(angles[...].reshape(GROUP, 128)))
        g.k_ref[h] = dk.astype(BF).reshape(4, 2, 128, 128)
        g.v_ref[h] = g.dv_t[...].T.astype(BF).reshape(4, 2, 128, 128)

    ring_c.on()

    def side(ref, zz):
        return [ref[h, :, zz].reshape(512, 128) for h in range(RANK_HEADS)]

    def first_parts(parts, zz, own_half):
        pieces = side(g.k_ref, zz) + side(g.v_ref, zz)
        if own_half:
            pieces = [g.q_ref[h].reshape(512, 128) for h in range(RANK_HEADS)] + pieces
        left = jnp.concatenate(pieces, axis=1)
        n = left.shape[1]
        to_parts(parts, left, lambda t: g.full_q[pl.ds(t * 2, 2), :, :, :, 1152 - n :].reshape(768, n), True, 2)

    first_parts(g.part_a, 1 - zh, False)
    ring_e = RingScatter(lines, lambda i: g.part_a.at[i], g.got_a, g.via_a)
    ring_e.start()
    scatter_u.second()
    ring_c.finish()
    block_out[...] = ring_c.total(g.middle[...] + g.part_c[x].astype(F32)).astype(BF)
    first_parts(g.part_c, zh, True)
    ring_f = RingScatter(lines, lambda i: g.part_c.at[i], g.got_b, g.via_b)
    ring_f.start()

    dq_all = jnp.concatenate([g.q_ref[h].reshape(512, 128) for h in range(RANK_HEADS)], axis=1)
    dkv_all = jnp.concatenate(
        [r[h].reshape(GROUP, 128) for r in (g.k_ref, g.v_ref) for h in range(RANK_HEADS)], axis=1
    )

    @pl.loop(0, 4)
    def _(t):
        mine = g.normed[:, zh, :, cols(t, 384)].reshape(512, 384)
        every = g.normed[:, :, :, cols(t, 384)].reshape(GROUP, 384)
        g.full_q[t, :, :, :, :RANK_COLS] = dot_tn(mine, dq_all).astype(BF).reshape(2, 2, 96, RANK_COLS)
        g.full_q[t, :, :, :, RANK_COLS:] = dot_tn(every, dkv_all).astype(BF).reshape(2, 2, 96, 768)

    scatter_q = [
        Scatter(lines, g.full_q, (g.sq0, g.sq1, g.sq2, g.sq3), 48, False, False, pl.ds(0, 640)),
        Scatter(lines, g.full_q, (g.sr0, g.sr1, g.sr2, g.sr3), 48, True, False, pl.ds(640, 512)),
    ]
    for t in scatter_q:
        t.cores()
    ring_e.on()
    scatter_d.second()
    d_out = dot_tn(g.att[...].reshape(512, RANK_COLS), branch_all).astype(BF)
    g.full_o[...] = pick(one_hot_rows(512, RANK_COLS, True), d_out).reshape(2, 2, 4, 32, D)
    scatter_o = Scatter(lines, g.full_o, (g.so0, g.so1, g.so2, g.so3), 16, True, True)
    scatter_o.cores()
    for t in scatter_q:
        t.first()
    ring_f.on()
    scatter_o.first()
    ring_e.finish()
    g.swap_out[...] = ring_e.total(g.part_a[x].astype(F32)).astype(BF)
    back = lines.copy(g.swap_out, g.swap_in, zh_peer())
    back.start()

    spread_rows = one_hot_rows(64, 48, True)
    g.got_u[...] = pick(spread_rows, scatter_u.total().astype(BF)).reshape(4, 16, D)
    plan_u = gather_home(lines, g.got_u, out_u)
    start_all(plan_u, g.got_u, out_u)
    for t in scatter_q:
        t.second()
    scatter_o.second()
    g.fin_d[...] = scatter_d.total().astype(BF)
    home_d = lines.copy(g.fin_d, out_d, swap_xy())
    home_o = lines.copy(g.fin_o, out_o, swap_xy())
    pl.when(x != y)(home_d.start)
    ring_f.finish()
    back.wait()
    h_one = ring_f.total(g.part_c[x].astype(F32)) + g.swap_in[...].astype(F32)
    grad_input[...] += rms_back(h_one, tokens[...].astype(F32))
    both = jnp.concatenate([scatter_q[0].total().astype(BF), scatter_q[1].total().astype(BF)], axis=1)
    g.got_q[...] = pick(spread_rows, both).reshape(4, 16, 1152)
    plan_q = gather_home(lines, g.got_q, out_q)
    start_all(plan_q, g.got_q, out_q)
    g.fin_o[...] = scatter_o.total().astype(BF)
    pl.when(x != y)(home_o.start)

    @pl.when(x == y)
    def _():
        out_o[...] = g.fin_o[...]
        out_d[...] = g.fin_d[...]

    wait_all(plan_u)

    @pl.when(x != y)
    def _():
        home_d.wait()
        home_o.wait()

    wait_all(plan_q)


def finish_kernel(
    block, grad, got_q, got_u, got_d, got_o, qkv, up, gain_one, gain_two,
    block_out, grad_input, d_gain_one, d_qkv, d_out, d_gain_two, d_up, d_down
):
    block_out[...] = block[...]
    grad_input[...] = grad[...]
    d_down[...] = got_d[...].astype(F32)
    d_out[...] = got_o[:12].astype(F32)
    one, two = column(gain_one[...].astype(F32)), column(gain_two[...].astype(F32))
    sum_one = sum_two = jnp.zeros((12, 1), F32)
    for i in range(4):
        for j in range(3):
            raw = got_q[i, :12, j * RANK_COLS : (j + 1) * RANK_COLS].astype(F32)
            at = j * D + i * RANK_COLS
            sum_one += jnp.sum(raw * qkv[:, at : at + RANK_COLS].astype(F32), axis=1, keepdims=True)
            d_qkv[:, at : at + RANK_COLS] = raw * one
        raw = got_u[i, :12].astype(F32)
        sum_two += jnp.sum(raw * up[:, i * D : (i + 1) * D].astype(F32), axis=1, keepdims=True)
        d_up[:, i * D : (i + 1) * D] = raw * two
    d_gain_one[...] = as_row(sum_one)
    d_gain_two[...] = as_row(sum_two)


def tables():
    inverse = np.exp(np.arange(64) * (-2.0 * math.log(10000.0) / HEAD_DIM))
    angles = np.arange(GROUP)[:, None] * inverse[None, :]
    return np.concatenate([np.cos(angles), np.sin(angles)], axis=1).astype(np.float32).reshape(4, 2, 128, 128)


def shapes_of(pairs):
    return [jax.ShapeDtypeStruct(s, t) for s, t in pairs]


def per_device(
    block_input, doc_lengths, ffn_levels, attn_gain, qkv_weight, out_weight, ffn_gain, up_weight, down_weight, grad_output
):
    vmem = pl.BlockSpec(memory_space=pltpu.VMEM)
    smem = pl.BlockSpec(memory_space=pltpu.SMEM)
    gain_one, gain_two = attn_gain.reshape(1, 12), ffn_gain.reshape(1, 12)
    outs = [((128, D), BF), ((128, D), F32), ((4, 16, 1152), BF), ((4, 16, D), BF), ((48, D), BF), ((16, D), BF)]
    made = pl.pallas_call(
        layer_kernel,
        out_shape=shapes_of(outs),
        in_specs=[smem] * 2 + [vmem] * 9,
        out_specs=[vmem] * len(outs),
        scratch_shapes=scratch_list(),
        compiler_params=pltpu.CompilerParams(collective_id=0, has_side_effects=True, vmem_limit_bytes=VMEM_LIMIT),
        name="layer_kernel",
    )(
        doc_lengths, ffn_levels, block_input[0], grad_output[0], qkv_weight, out_weight, up_weight, down_weight,
        gain_one, gain_two, jnp.asarray(tables()),
    )
    outs = [((128, D), BF), ((128, D), F32), ((1, 12), F32), ((12, 3 * D), F32), ((12, D), F32), ((1, 12), F32)]
    outs += [((12, FF), F32), ((48, D), F32)]
    block, grad, d_gain_one, d_qkv, d_out, d_gain_two, d_up, d_down = pl.pallas_call(
        finish_kernel,
        out_shape=shapes_of(outs),
        in_specs=[vmem] * 10,
        out_specs=[vmem] * len(outs),
        compiler_params=pltpu.CompilerParams(vmem_limit_bytes=VMEM_LIMIT),
        name="finish_kernel",
    )(*made, qkv_weight, up_weight, gain_one, gain_two)
    return block[None], grad[None], d_gain_one.reshape(12), d_qkv, d_out, d_gain_two.reshape(12), d_up, d_down


def solution(mesh):
    rows = P("batch", "seq", None)
    every = ("batch", "seq")
    return jax.shard_map(
        per_device,
        mesh=mesh,
        in_specs=(rows, P("batch", None), P("batch", None), P(every), P(every, None), P(every, None), P(every),
                  P(every, None), P(every, None), rows),
        out_specs=(rows, rows, P(every), P(every, None), P(every, None), P(every), P(every, None), P(every, None)),
        check_vma=False,
    )
```

```python
import math

import jax
import jax.numpy as jnp
import numpy as np
from jax import lax
from jax.experimental import pallas as pl
from jax.experimental.pallas import tpu as pltpu
from jax.sharding import PartitionSpec as P

HEADS = 12
HEAD_DIM = 128
D = 1536
FF = 6144
DOCS = 6
GROUP = 1024
SHARD = 128
RANK_HEADS = 3
RANK_COLS = 384
EPS = 1e-06
VMEM_LIMIT = 63 * 2**20
BF = jnp.bfloat16
F32 = jnp.float32
MESH = pl.DeviceIdType.MESH


def coords():
    b = lax.axis_index("batch")
    s = lax.axis_index("seq")
    return b // 4, (b // 2) % 2, b % 2, s // 2, s % 2


def dev(y, zl, c, x, zh):
    return (y * 4 + zl * 2 + c, x * 2 + zh)


def x_peers():
    y, zl, c, x, zh = coords()
    return [dev(y, zl, c, (x + k) % 4, zh) for k in (1, 2, 3)]


def y_peers():
    y, zl, c, x, zh = coords()
    return [dev((y + k) % 4, zl, c, x, zh) for k in (1, 2, 3)]


def z_peers():
    y, zl, c, x, zh = coords()
    z = zh * 2 + zl
    return [dev(y, (z + k) % 2, c, x, ((z + k) % 4) // 2) for k in (1, 2, 3)]


def core_peer():
    y, zl, c, x, zh = coords()
    return dev(y, zl, 1 - c, x, zh)


def zh_peer():
    y, zl, c, x, zh = coords()
    return dev(y, zl, c, x, 1 - zh)


class Lines:
    def __init__(self, send, recv):
        self.send, self.recv, self.used = send, recv, 0

    def copy(self, src, dst, peer):
        at = self.used
        self.used += 1
        return pltpu.make_async_remote_copy(
            src, dst, self.send.at[at], self.recv.at[at], device_id=peer, device_id_type=MESH
        )


LO, HI = pl.ds(0, 64), pl.ds(64, 64)


def ring(axis):
    y, zl, c, x, zh = coords()
    if axis == "x":
        return x, x_peers()[0], x_peers()[2]
    if axis == "y":
        return y, y_peers()[0], y_peers()[2]
    return zh * 2 + zl, z_peers()[0], z_peers()[2]


class RingGather:
    def __init__(self, lines, axis, lo, hi):
        self.lines, self.axis, self.lo, self.hi = lines, axis, lo, hi

    def start(self):
        me, nxt, prv = ring(self.axis)
        lo, hi = self.lo(me), self.hi(me)
        self.first = self.lines.copy(lo, lo, nxt)
        self.second = self.lines.copy(hi, hi, prv)
        self.rest = [self.lines.copy(hi, hi, nxt), self.lines.copy(lo, lo, prv)]
        for cp in (self.first, self.second, *self.rest):
            cp.start()

    def on(self):
        me, nxt, prv = ring(self.axis)
        lo, hi = self.lo((me + 3) % 4), self.hi((me + 1) % 4)
        self.first.wait_recv()
        one = self.lines.copy(lo, lo, nxt)
        one.start()
        self.second.wait_recv()
        two = self.lines.copy(hi, hi, prv)
        two.start()
        self.rest += [one, two]

    def finish(self):
        self.first.wait_send()
        self.second.wait_send()
        for cp in self.rest:
            cp.wait()


class RingScatter:
    def __init__(self, lines, axis, lo, hi, got, via):
        self.lines, self.axis, self.lo, self.hi, self.got, self.via = lines, axis, lo, hi, got, via

    def start(self):
        me, nxt, prv = ring(self.axis)
        left, right, far = (me + 3) % 4, (me + 1) % 4, (me + 2) % 4
        self.far_lo = self.lines.copy(self.lo(far), self.via.at[0], nxt)
        self.far_hi = self.lines.copy(self.hi(far), self.via.at[1], prv)
        self.rest = [
            self.lines.copy(self.hi(right), self.got.at[2], nxt),
            self.lines.copy(self.lo(left), self.got.at[0], prv),
        ]
        for cp in (self.far_lo, self.far_hi, *self.rest):
            cp.start()

    def on(self):
        me, nxt, prv = ring(self.axis)
        left, right = (me + 3) % 4, (me + 1) % 4
        via = self.via
        self.far_lo.wait_recv()
        via[0] = (via[0].astype(F32) + self.lo(right)[...].astype(F32)).astype(BF)
        one = self.lines.copy(via.at[0], self.got.at[1], nxt)
        one.start()
        self.far_hi.wait_recv()
        via[1] = (via[1].astype(F32) + self.hi(left)[...].astype(F32)).astype(BF)
        two = self.lines.copy(via.at[1], self.got.at[3], prv)
        two.start()
        self.rest += [one, two]

    def finish(self):
        self.far_lo.wait_send()
        self.far_hi.wait_send()
        for cp in self.rest:
            cp.wait()

    def others(self):
        got = self.got
        return got[0].astype(F32) + got[1].astype(F32), got[2].astype(F32) + got[3].astype(F32)

    def total(self, own):
        return own + jnp.concatenate(self.others(), axis=0)


def gather_x(lines, place):
    return RingGather(lines, "x", lambda i: place(i, LO), lambda i: place(i, HI))


def scatter_x(lines, parts, got, via):
    return RingScatter(lines, "x", lambda i: parts.at[i, LO], lambda i: parts.at[i, HI], got, via)


def one_hot_rows(rows, cols, expand):
    i = lax.broadcasted_iota(jnp.int32, (rows, cols), 0)
    j = lax.broadcasted_iota(jnp.int32, (rows, cols), 1)
    a, p = (j, i) if expand else (i, j)
    return jnp.where((p % 16 < 12) & (p // 16 * 12 + p % 16 == a), 1.0, 0.0).astype(BF)


def pick(matrix, values):
    return jnp.dot(matrix, values, preferred_element_type=F32).astype(BF)


def seq_peers():
    y, zl, c, x, zh = coords()
    s = x * 2 + zh
    found = []
    for k in range(1, 8):
        t = (s + k) % 8
        found.append(dev(y, zl, c, t // 2, t % 2))
    return found


def greet():
    y, _, _, x, _ = coords()
    sem = pltpu.get_barrier_semaphore()
    peers = seq_peers() + y_peers() + z_peers()[::2] + [core_peer()]
    for peer in peers:
        pl.semaphore_signal(sem, inc=1, device_id=peer, device_id_type=MESH)

    @pl.when(x != y)
    def _():
        pl.semaphore_signal(sem, inc=1, device_id=swap_xy(), device_id_type=MESH)

    return len(peers) + jnp.where(x != y, 1, 0)


def swap_xy():
    y, zl, c, x, zh = coords()
    return dev(x, zl, c, y, zh)


def spread(lines, src, dst):
    y, zl, c, x, zh = coords()
    s = x * 2 + zh
    at = lines.used
    lines.used += 4
    sends, arrivals = [], []
    for k in range(4):
        i = (x + k) % 4
        own = (i == x) & (x // 2 == zh)
        cp = pltpu.make_async_remote_copy(
            src.at[i], dst.at[s % 4], lines.send.at[at + k], lines.recv.at[at + s % 4],
            device_id=dev(y, zl, c, i, x // 2), device_id_type=MESH,
        )
        sends.append((cp, own))
    for j in range(4):
        own = (x // 2 == zh) & (s % 4 == j)
        cp = pltpu.make_async_remote_copy(
            src.at[j], dst.at[j], lines.send.at[at], lines.recv.at[at + j],
            device_id=core_peer(), device_id_type=MESH,
        )
        arrivals.append((cp, own))
    return sends, arrivals, (x // 2 == zh), x, s % 4


def gather_home(lines, src, dst):
    y, zl, c, x, zh = coords()
    s = x * 2 + zh
    at = lines.used
    lines.used += 4
    sends, arrivals = [], []
    for k in range(4):
        i = (s + k) % 4
        t = 4 * zh + i
        own = t == s
        cp = pltpu.make_async_remote_copy(
            src.at[i], dst.at[x], lines.send.at[at + k], lines.recv.at[at + x],
            device_id=dev(y, zl, c, t // 2, t % 2), device_id_type=MESH,
        )
        sends.append((cp, own))
    for j in range(4):
        own = (x // 2 == zh) & (x == j)
        cp = pltpu.make_async_remote_copy(
            src.at[j], dst.at[j], lines.send.at[at], lines.recv.at[at + j],
            device_id=core_peer(), device_id_type=MESH,
        )
        arrivals.append((cp, own))
    return sends, arrivals, (x // 2 == zh), s % 4, x


def start_all(plan, src, dst):
    sends, _, mine, from_slot, to_slot = plan
    for cp, own in sends:
        pl.when(jnp.logical_not(own))(cp.start)

    @pl.when(mine)
    def _():
        dst[to_slot] = src[from_slot]


def wait_all(plan):
    sends, arrivals = plan[:2]
    for cp, own in arrivals:
        pl.when(jnp.logical_not(own))(cp.wait_recv)
    for cp, own in sends:
        pl.when(jnp.logical_not(own))(cp.wait_send)


class Gather:
    def __init__(self, lines, full, rows, z_first, y_inner=False, columns=None):
        self.lines, self.full, self.rows, self.z_first, self.y_inner = lines, full, rows, z_first, y_inner
        self.columns = pl.ds(0, full.shape[-1]) if columns is None else columns
        self.pending = []

    def _at(self, y, zl, c, rows):
        place = (zl, c, y) if self.y_inner else (y, zl, c)
        return self.full.at[(*place, rows, self.columns)]

    def _send(self, src, peers):
        copies = [self.lines.copy(src, src, p) for p in peers]
        for cp in copies:
            cp.start()
        self.pending = copies

    def near(self):
        y, zl, c, _, zh = coords()
        mine = self._at(y, zl, c, pl.ds(zh * self.rows, self.rows))
        self._send(mine, z_peers() if self.z_first else y_peers())

    def wide(self):
        self.wait()
        y, zl, c, _, zh = coords()
        if self.z_first:
            rows = pl.ds(0, 2 * self.rows)
            self.ring = RingGather(
                self.lines, "y", lambda i: self._at(i, 0, c, rows), lambda i: self._at(i, 1, c, rows)
            )
        else:
            rows = lambda i: pl.ds(i // 2 * self.rows, self.rows)
            self.ring = RingGather(
                self.lines, "z", lambda i: self._at(pl.ds(0, 2), i % 2, c, rows(i)),
                lambda i: self._at(pl.ds(2, 2), i % 2, c, rows(i)),
            )
        self.ring.start()

    def on(self):
        self.ring.on()

    def cores(self):
        self.ring.finish()
        c = coords()[2]
        self._send(self._at(slice(None), slice(None), c, pl.ds(0, 2 * self.rows)), [core_peer()])

    def wait(self):
        for cp in self.pending:
            cp.wait()
        self.pending = []


class Scatter:
    def __init__(self, lines, part, bufs, rows, y_first, y_inner=False, columns=None):
        self.lines, self.part = lines, part
        self.half, self.got, self.via, self.wide, self.wide_in = bufs
        self.rows, self.y_first, self.y_inner, self.pending = rows, y_first, y_inner, []
        self.columns = pl.ds(0, part.shape[-1]) if columns is None else columns

    def wait(self):
        for cp in self.pending:
            cp.wait()
        self.pending = []

    def _start(self, copies):
        for cp in copies:
            cp.start()
        self.pending = copies

    def cores(self):
        c = coords()[2]
        rows = pl.ds(0, 2 * self.rows)
        place = (slice(None), 1 - c, slice(None)) if self.y_inner else (slice(None), slice(None), 1 - c)
        self._start([self.lines.copy(self.part.at[(*place, rows, self.columns)], self.half, core_peer())])

    def _block(self, side, i):
        if not self.y_first:
            rows, pair = pl.ds(i // 2 * self.rows, self.rows), pl.ds(2 * side, 2)
            return self.half.at[i % 2, pair, rows] if self.y_inner else self.half.at[pair, i % 2, rows]
        return self.half.at[side, i] if self.y_inner else self.half.at[i, side]

    def first(self):
        self.wait()
        c, inner = coords()[2], self.half.shape[1]

        @pl.loop(0, 8)
        def _(i):
            a, b = i // inner, i % inner
            place = (a, c, b) if self.y_inner else (a, b, c)
            both = self.part[(*place, slice(None), self.columns)].astype(F32) + self.half[a, b].astype(F32)
            self.half[a, b] = both.astype(BF)

        self.ring = RingScatter(
            self.lines, "y" if self.y_first else "z", lambda i: self._block(0, i), lambda i: self._block(1, i),
            self.got, self.via,
        )
        self.ring.start()

    def on(self):
        self.ring.on()

    def second(self):
        self.ring.finish()
        me = ring("y" if self.y_first else "z")[0]
        for side, others in enumerate(self.ring.others()):
            self.wide[side] = (self._block(side, me)[...].astype(F32) + others).astype(BF)
        copies = []
        for k in (1, 2, 3):
            peer = (z_peers if self.y_first else y_peers)()[k - 1]
            copies.append(self.lines.copy(self._piece(k), self.wide_in.at[k - 1], peer))
        self._start(copies)

    def _piece(self, k):
        y, zl, c, _, zh = coords()
        if self.y_first:
            zz = (zh * 2 + zl + k) % 4
            return self.wide.at[zz % 2, pl.ds(zz // 2 * self.rows, self.rows)]
        yy = (y + k) % 4
        return self.wide.at[yy // 2, yy % 2]

    def total(self):
        self.wait()
        total = self._piece(0)[...].astype(F32)
        for k in range(3):
            total += self.wide_in[k].astype(F32)
        return total


class Both:
    def __init__(self, lines, part, bufs, rows, split, width, y_inner=False):
        n = len(bufs) // 2
        self.parts = [
            Scatter(lines, part, bufs[:n], rows, False, y_inner, pl.ds(0, split)),
            Scatter(lines, part, bufs[n:], rows, True, y_inner, pl.ds(split, width - split)),
        ]

    def __getattr__(self, step):
        return lambda: [getattr(p, step)() for p in self.parts]

    def sums(self):
        return jnp.concatenate([p.total().astype(BF) for p in self.parts], axis=1)


def scatter_scratch(rows, split, width, y_inner=False):
    found = []
    for n, y_first in ((split, False), (width - split, True)):
        half = (2, 4, 2 * rows, n) if y_inner else (4, 2, 2 * rows, n)
        block = (2 * rows, n) if y_first else (2, rows, n)
        found += [pltpu.VMEM(s, BF) for s in (half, (4, *block), (2, *block), (2, *block), (3, rows, n))]
    return found


def dot(a, b):
    return jnp.dot(a, b, preferred_element_type=F32)


def dot_nt(a, b):
    return lax.dot_general(a, b, (((1,), (1,)), ((), ())), preferred_element_type=F32)


def dot_tn(a, b):
    return lax.dot_general(a, b, (((0,), (0,)), ((), ())), preferred_element_type=F32)


def normalize(values):
    r = lax.rsqrt(jnp.mean(values * values, axis=-1, keepdims=True) + EPS)
    return r, values * r


def rms_back(grad, values):
    r, hat = normalize(values)
    return r * (grad - hat * jnp.mean(grad * hat, axis=-1, keepdims=True))


def cos_sin(table):
    other = pltpu.roll(table, 64, 1)
    low = lax.broadcasted_iota(jnp.int32, table.shape, 1) < 64
    return jnp.where(low, table, other), jnp.where(low, -other, table)


def turn(v, cos, sin):
    return v * cos + pltpu.roll(v, 64, 1) * sin


def turn_back(v, cos, sin):
    return v * cos - pltpu.roll(v, 64, 1) * sin


GELU_A, GELU_B = math.sqrt(2.0 / math.pi), 0.044715


def gelu_both(v):
    square = v * v
    t = jnp.tanh(GELU_A * v * (1.0 + GELU_B * square))
    half = 0.5 * (1.0 + t)
    return v * half, half + 0.5 * v * (1.0 - t * t) * (GELU_A * (1.0 + 3.0 * GELU_B * square))


def cols(i, n):
    return pl.ds(pl.multiple_of(i * n, n), n)


NAMES = (
    "full_q", "full_u", "full_d", "full_o", "got_q", "got_u", "src_q", "src_u", "src_o",
    "normed", "q_ref", "k_ref", "v_ref", "p0", "p1", "p2", "p3",
    "att", "att_grad", "middle", "wo", "ntwo", "up_grad", "hidden", "pre_grad", "branch", "part_a", "part_c",
    "got_a", "via_a", "got_b", "via_b", "got_c", "via_c", "swap_out", "swap_in", "dk_t", "dv_t",
    *(f"s{w}{k}" for w in "qudo" for k in range(10)), "fin_o", "fin_d", "send", "recv",
)


def scratch_list():
    V = pltpu.VMEM
    block = V((4, 128, D), BF)
    got, via = V((4, 64, D), BF), V((2, 64, D), BF)
    kv = V((3, 4, 2, 128, 128), BF)
    shapes = [V((4, 2, 2, 96, 1152), BF), V((4, 2, 2, 96, D), BF), V((2, 2, 4, 96, D), BF), V((2, 2, 4, 32, D), BF)]
    shapes += [V((4, 16, 1152), BF), V((4, 16, D), BF)] * 2 + [V((16, D), BF)]
    shapes += [V((4, 2, 128, D), BF), V((3, 4, 128, 128), BF), kv, kv]
    shapes += [V((3, 128, 256 * (i + 1)), BF) for i in range(4)]
    shapes += [V((4, 128, RANK_COLS), BF), V((4, 128, RANK_COLS), BF), V((128, D), F32), V((RANK_COLS, D), BF)]
    shapes += [block] * 7
    shapes += [got, via] * 3 + [V((128, D), BF), V((128, D), BF)]
    shapes += [V((128, GROUP), F32), V((128, GROUP), F32)]
    shapes += scatter_scratch(48, 640, 1152) + scatter_scratch(48, 768, D)
    shapes += scatter_scratch(48, 768, D, True) + scatter_scratch(16, 768, D, True)
    shapes += [V((16, D), BF), V((48, D), BF)]
    shapes += [pltpu.SemaphoreType.DMA((300,)), pltpu.SemaphoreType.DMA((300,))]
    assert len(shapes) == len(NAMES)
    return shapes


class Refs:
    pass


def column(row):
    n = row.shape[1]
    same = lax.broadcasted_iota(jnp.int32, (n, n), 0) == lax.broadcasted_iota(jnp.int32, (n, n), 1)
    return jnp.sum(jnp.where(same, row, 0.0), axis=1, keepdims=True)


def as_row(col):
    n = col.shape[0]
    same = lax.broadcasted_iota(jnp.int32, (n, n), 0) == lax.broadcasted_iota(jnp.int32, (n, n), 1)
    return jnp.sum(jnp.where(same, col, 0.0), axis=0, keepdims=True)


def sixteen(rows):
    return jnp.concatenate([rows, jnp.zeros((4, rows.shape[1]), rows.dtype)], axis=0).astype(BF)


def documents(lengths, levels, positions):
    start, width = jnp.zeros_like(positions), jnp.zeros_like(positions)
    first = 0
    for d in range(DOCS):
        level = levels[0, d]
        wide = jnp.where(level == 0, FF // 8, jnp.where(level == 1, FF // 4, jnp.where(level == 2, FF // 2, FF)))
        inside = positions >= first
        start = jnp.where(inside, first, start)
        width = jnp.where(inside, wide, width)
        first = first + lengths[0, d]
    return start, width


def layer_kernel(
    lengths, levels, tokens, grad_in, qkv, out_w, up, down, gain_one, gain_two, angles,
    block_out, grad_input, out_q, out_u, out_d, out_o, *scratch
):
    g = Refs()
    for name, ref in zip(NAMES, scratch):
        setattr(g, name, ref)
    bufs = lambda w: [getattr(g, f"s{w}{k}") for k in range(10)]
    y, zl, c, x, zh = coords()
    lines = Lines(g.send, g.recv)
    scale = HEAD_DIM**-0.5
    greetings = greet()

    g.normed[x, zh] = normalize(tokens[...].astype(F32))[1].astype(BF)
    g.up_grad[x] = grad_in[...]
    one, two = column(gain_one[...].astype(F32)), column(gain_two[...].astype(F32))
    for i in range(4):
        for j in range(3):
            at = j * D + i * RANK_COLS
            g.src_q[i, :, j * RANK_COLS : (j + 1) * RANK_COLS] = sixteen(qkv[:, at : at + RANK_COLS].astype(F32) * one)
        g.src_u[i] = sixteen(up[:, i * D : (i + 1) * D].astype(F32) * two)
    g.src_o[...] = sixteen(out_w[...].astype(F32))
    pl.semaphore_wait(pltpu.get_barrier_semaphore(), greetings)

    ring_one = gather_x(lines, lambda i, h: g.normed.at[i, zh, h])
    ring_two = gather_x(lines, lambda i, h: g.normed.at[i, 1 - zh, h])
    swap = lines.copy(g.normed.at[x, zh], g.normed.at[x, zh], zh_peer())
    plan_q = spread(lines, g.src_q, g.got_q)
    start_all(plan_q, g.src_q, g.got_q)
    swap_o = lines.copy(g.src_o, g.full_o.at[zl, c, x, pl.ds(zh * 16, 16)], swap_xy())
    swap_d = lines.copy(down, g.full_d.at[zl, c, x, pl.ds(zh * 48, 48)], swap_xy())
    ring_one.start()
    swap.start()
    pl.when(x != y)(swap_o.start)
    rows = one_hot_rows(48, 64, False)
    wait_all(plan_q)
    g.full_q[y, zl, c, pl.ds(zh * 48, 48)] = pick(rows, g.got_q[...].reshape(64, 1152))
    gather_q = [
        Gather(lines, g.full_q, 48, True, False, pl.ds(0, 640)),
        Gather(lines, g.full_q, 48, False, False, pl.ds(640, 512)),
    ]
    gather_o = Gather(lines, g.full_o, 16, False, True)
    gather_u = Gather(lines, g.full_u, 48, True)
    gather_d = Gather(lines, g.full_d, 48, False, True)
    for t in gather_q:
        t.near()

    @pl.when(x == y)
    def _():
        g.full_o[zl, c, x, pl.ds(zh * 16, 16)] = g.src_o[...]
        g.full_d[zl, c, x, pl.ds(zh * 48, 48)] = down[...]

    ring_one.on()
    pl.when(x != y)(swap_o.wait)
    gather_o.near()
    swap.wait_recv()
    ring_two.start()
    plan_u = spread(lines, g.src_u, g.got_u)
    start_all(plan_u, g.src_u, g.got_u)
    pl.when(x != y)(swap_d.start)
    for t in (*gather_q, gather_o):
        t.wide()
    for t in (*gather_q, gather_o):
        t.on()
    ring_two.on()
    for t in gather_q:
        t.cores()
    wait_all(plan_u)
    g.full_u[y, zl, c, pl.ds(zh * 48, 48)] = pick(rows, g.got_u[...].reshape(64, D))
    gather_u.near()
    gather_o.cores()
    ring_one.finish()
    for t in gather_q:
        t.wait()

    def project(zz, own_half):
        block = g.normed[:, zz].reshape(512, D)
        cos_b, sin_b = cos_sin(angles[:, zz].reshape(512, 128))
        for j in range(0 if own_half else 1, 3):
            made = dot(block, g.full_q[:, :, :, :, j * RANK_COLS : (j + 1) * RANK_COLS].reshape(D, RANK_COLS))
            for h in range(RANK_HEADS):
                head = made[:, h * 128 : (h + 1) * 128]
                if j < 2:
                    head = turn(head, cos_b, sin_b)
                head = head.astype(BF).reshape(4, 128, 128)
                if j == 0:
                    g.q_ref[h] = head
                elif j == 1:
                    g.k_ref[h, :, zz] = head
                else:
                    g.v_ref[h, :, zz] = head

    project(zh, True)
    pl.when(x != y)(swap_d.wait)
    gather_d.near()
    ring_two.finish()
    swap.wait_send()
    ring_up = gather_x(lines, lambda i, h: g.up_grad.at[i, h])
    ring_up.start()
    project(1 - zh, False)
    gather_u.wide()
    gather_d.wide()

    probs = [g.p0, g.p1, g.p2, g.p3]

    @pl.loop(0, RANK_HEADS)
    def _(h):
        for i in range(4):
            n = 256 * (i + 1)
            keys = g.k_ref[h, : i + 1].reshape(n, 128)
            values = g.v_ref[h, : i + 1].reshape(n, 128)
            scores = dot_nt(g.q_ref[h, i], keys) * scale
            base = (2 * i + zh) * 128
            q_at = base + lax.broadcasted_iota(jnp.int32, (128, n), 0)
            k_at = lax.broadcasted_iota(jnp.int32, (128, n), 1)
            first = documents(lengths, levels, base + lax.broadcasted_iota(jnp.int32, (128, 1), 0))[0]
            scores = jnp.where((k_at <= q_at) & (k_at >= first), scores, -1e30)
            e = jnp.exp(scores - jnp.max(scores, axis=-1, keepdims=True))
            p = (e * (1.0 / jnp.sum(e, axis=-1, keepdims=True))).astype(BF)
            probs[i][h] = p
            g.att[i, :, pl.ds(pl.multiple_of(h * 128, 128), 128)] = dot(p, values).astype(BF)

    ring_up.on()
    gather_o.wait()
    g.wo[...] = pick(one_hot_rows(RANK_COLS, 512, False), g.full_o[...].reshape(512, D))

    def to_parts(parts, left, right_of, transposed, tiles):
        n = D // tiles

        @pl.loop(0, tiles)
        def _(t):
            right = right_of(t)
            made = dot_nt(left, right) if transposed else dot(left, right)
            parts[:, :, cols(t, n)] = made.astype(BF).reshape(4, 128, n)

    to_parts(g.part_a, g.att[...].reshape(512, RANK_COLS), lambda t: g.wo[:, cols(t, 512)], False, 3)
    ring_a = scatter_x(lines, g.part_a, g.got_a, g.via_a)
    ring_a.start()
    gather_u.on()
    gather_d.on()
    ring_up.finish()
    ring_a.on()
    ring_a.finish()
    g.middle[...] = ring_a.total(tokens[...].astype(F32) + g.part_a[x].astype(F32))
    g.ntwo[x] = normalize(g.middle[...])[1].astype(BF)
    ring_n = gather_x(lines, lambda i, h: g.ntwo.at[i, h])
    ring_n.start()
    gather_d.cores()
    gather_u.cores()
    ring_n.on()

    def full_rows(ref, t):
        return ref[pl.ds(t * 2, 2)].reshape(768, ref.shape[-1])

    def full_cols(ref, t, n):
        return ref[:, :, :, :, cols(t, n)].reshape(D, n)

    gather_d.wait()
    up_all = g.up_grad[...].reshape(512, D)
    to_parts(g.pre_grad, up_all, lambda t: g.full_d[t].reshape(768, D), True, 2)
    gather_u.wait()
    ring_n.finish()

    width = jnp.concatenate(
        [
            documents(lengths, levels, (2 * i + zh) * 128 + lax.broadcasted_iota(jnp.int32, (128, 1), 0))[1]
            for i in range(4)
        ],
        axis=0,
    )

    @pl.loop(0, 6)
    def _(t):
        pre = dot(g.ntwo[...].reshape(512, D), full_cols(g.full_u, t, 256))
        unit = x * D + t * 256 + lax.broadcasted_iota(jnp.int32, (512, 256), 1)
        mask = unit < width
        act, slope = gelu_both(pre)
        g.hidden[:, :, cols(t, 256)] = jnp.where(mask, act, 0.0).astype(BF).reshape(4, 128, 256)
        back = g.pre_grad[:, :, cols(t, 256)].reshape(512, 256).astype(F32)
        g.pre_grad[:, :, cols(t, 256)] = jnp.where(mask, slope * back, 0.0).astype(BF).reshape(4, 128, 256)

    pre_all = g.pre_grad[...].reshape(512, D)
    to_parts(g.part_a, pre_all, lambda t: full_rows(g.full_u, t), True, 2)
    ring_b = scatter_x(lines, g.part_a, g.got_b, g.via_b)
    ring_b.start()

    def weight_grad(full, left_of, right):
        @pl.loop(0, 4)
        def _(t):
            made = dot_tn(left_of(t), right).astype(BF)
            if full.shape[0] == 4:
                full[t] = made.reshape(full.shape[1:])
            else:
                full[t // 2, t % 2] = made.reshape(full.shape[2:])

    weight_grad(g.full_u, lambda t: g.ntwo[:, :, cols(t, 384)].reshape(512, 384), pre_all)
    scatter_u = Both(lines, g.full_u, bufs("u"), 48, 768, D)
    scatter_u.cores()
    ring_b.on()
    to_parts(g.part_c, g.hidden[...].reshape(512, D), lambda t: full_cols(g.full_d, t, 512), False, 3)
    scatter_u.first()
    weight_grad(g.full_d, lambda t: g.hidden[:, :, cols(t, 384)].reshape(512, 384), up_all)
    scatter_d = Both(lines, g.full_d, bufs("d"), 48, 768, D, True)
    scatter_d.cores()
    ring_b.finish()

    grad_input[...] = grad_in[...].astype(F32) + rms_back(ring_b.total(g.part_a[x].astype(F32)), g.middle[...])
    g.branch[x] = grad_input[...].astype(BF)
    ring_g = gather_x(lines, lambda i, h: g.branch.at[i, h])
    ring_g.start()
    scatter_u.on()
    ring_g.on()
    scatter_d.first()
    ring_g.finish()
    ring_c = scatter_x(lines, g.part_c, g.got_c, g.via_c)
    ring_c.start()

    branch_all = g.branch[...].reshape(512, D)
    scatter_u.second()
    g.att_grad[...] = dot_nt(branch_all, g.wo[...]).astype(BF).reshape(4, 128, RANK_COLS)
    d_out = dot_tn(g.att[...].reshape(512, RANK_COLS), branch_all).astype(BF)
    g.full_o[...] = pick(one_hot_rows(512, RANK_COLS, True), d_out).reshape(2, 2, 4, 32, D)
    scatter_o = Both(lines, g.full_o, bufs("o"), 16, 768, D, True)
    scatter_o.cores()

    @pl.loop(0, RANK_HEADS)
    def _(h):
        at = pl.ds(pl.multiple_of(h * 128, 128), 128)
        g.dk_t[...] = jnp.zeros_like(g.dk_t)
        g.dv_t[...] = jnp.zeros_like(g.dv_t)
        for i in range(4):
            n = 256 * (i + 1)
            keys = g.k_ref[h, : i + 1].reshape(n, 128)
            values = g.v_ref[h, : i + 1].reshape(n, 128)
            queries = g.q_ref[h, i]
            p = probs[i][h]
            grad = g.att_grad[i, :, at]
            delta = jnp.sum(grad.astype(F32) * g.att[i, :, at].astype(F32), axis=-1, keepdims=True)
            ds = (p.astype(F32) * (dot_nt(grad, values) - delta)).astype(BF)
            dq = dot(ds, keys) * scale
            g.dk_t[:, :n] += dot(queries.T, ds)
            g.dv_t[:, :n] += dot(grad.T, p)
            g.q_ref[h, i] = turn_back(dq, *cos_sin(angles[i, zh])).astype(BF)
        dk = g.dk_t[...].T * scale
        dk = turn_back(dk, *cos_sin(angles[...].reshape(GROUP, 128)))
        g.k_ref[h] = dk.astype(BF).reshape(4, 2, 128, 128)
        g.v_ref[h] = g.dv_t[...].T.astype(BF).reshape(4, 2, 128, 128)

    ring_c.on()
    scatter_d.on()
    scatter_o.first()

    def side(ref, zz):
        return [ref[h, :, zz].reshape(512, 128) for h in range(RANK_HEADS)]

    def first_parts(parts, zz, own_half):
        pieces = side(g.k_ref, zz) + side(g.v_ref, zz)
        if own_half:
            pieces = [g.q_ref[h].reshape(512, 128) for h in range(RANK_HEADS)] + pieces
        left = jnp.concatenate(pieces, axis=1)
        n = left.shape[1]
        to_parts(parts, left, lambda t: g.full_q[pl.ds(t * 2, 2), :, :, :, 1152 - n :].reshape(768, n), True, 2)

    first_parts(g.part_a, 1 - zh, False)
    ring_e = scatter_x(lines, g.part_a, g.got_a, g.via_a)
    ring_e.start()
    first_parts(g.ntwo, zh, True)
    ring_f = scatter_x(lines, g.ntwo, g.got_b, g.via_b)
    ring_f.start()

    dq_all = jnp.concatenate([g.q_ref[h].reshape(512, 128) for h in range(RANK_HEADS)], axis=1)
    dkv_all = jnp.concatenate(
        [r[h].reshape(GROUP, 128) for r in (g.k_ref, g.v_ref) for h in range(RANK_HEADS)], axis=1
    )

    @pl.loop(0, 4)
    def _(t):
        mine = g.normed[:, zh, :, cols(t, 384)].reshape(512, 384)
        every = g.normed[:, :, :, cols(t, 384)].reshape(GROUP, 384)
        g.full_u[t, :, :, :, :RANK_COLS] = dot_tn(mine, dq_all).astype(BF).reshape(2, 2, 96, RANK_COLS)
        g.full_u[t, :, :, :, RANK_COLS:1152] = dot_tn(every, dkv_all).astype(BF).reshape(2, 2, 96, 768)

    scatter_q = Both(lines, g.full_u, bufs("q"), 48, 640, 1152)
    scatter_q.cores()
    ring_e.on()
    scatter_d.second()
    scatter_q.first()
    scatter_o.on()
    ring_c.finish()
    block_out[...] = ring_c.total(g.middle[...] + g.part_c[x].astype(F32)).astype(BF)
    spread_rows = one_hot_rows(64, 48, True)
    g.got_u[...] = pick(spread_rows, scatter_u.sums()).reshape(4, 16, D)
    plan_u = gather_home(lines, g.got_u, out_u)
    start_all(plan_u, g.got_u, out_u)
    ring_f.on()
    scatter_q.on()
    scatter_o.second()
    ring_e.finish()
    g.swap_out[...] = ring_e.total(g.part_a[x].astype(F32)).astype(BF)
    back = lines.copy(g.swap_out, g.swap_in, zh_peer())
    back.start()
    scatter_q.second()
    g.fin_d[...] = scatter_d.sums()
    home_d = lines.copy(g.fin_d, out_d, swap_xy())
    home_o = lines.copy(g.fin_o, out_o, swap_xy())
    pl.when(x != y)(home_d.start)
    g.fin_o[...] = scatter_o.sums()
    pl.when(x != y)(home_o.start)

    g.got_q[...] = pick(spread_rows, scatter_q.sums()).reshape(4, 16, 1152)
    plan_q = gather_home(lines, g.got_q, out_q)
    start_all(plan_q, g.got_q, out_q)
    ring_f.finish()
    back.wait()
    h_one = ring_f.total(g.ntwo[x].astype(F32)) + g.swap_in[...].astype(F32)
    grad_input[...] += rms_back(h_one, tokens[...].astype(F32))

    @pl.when(x == y)
    def _():
        out_o[...] = g.fin_o[...]
        out_d[...] = g.fin_d[...]

    wait_all(plan_u)

    @pl.when(x != y)
    def _():
        home_d.wait()
        home_o.wait()

    wait_all(plan_q)


def finish_kernel(
    block, grad, got_q, got_u, got_d, got_o, qkv, up, gain_one, gain_two,
    block_out, grad_input, d_gain_one, d_qkv, d_out, d_gain_two, d_up, d_down
):
    block_out[...] = block[...]
    grad_input[...] = grad[...]
    d_down[...] = got_d[...].astype(F32)
    d_out[...] = got_o[:12].astype(F32)
    one, two = column(gain_one[...].astype(F32)), column(gain_two[...].astype(F32))
    sum_one = sum_two = jnp.zeros((12, 1), F32)
    for i in range(4):
        for j in range(3):
            raw = got_q[i, :12, j * RANK_COLS : (j + 1) * RANK_COLS].astype(F32)
            at = j * D + i * RANK_COLS
            sum_one += jnp.sum(raw * qkv[:, at : at + RANK_COLS].astype(F32), axis=1, keepdims=True)
            d_qkv[:, at : at + RANK_COLS] = raw * one
        raw = got_u[i, :12].astype(F32)
        sum_two += jnp.sum(raw * up[:, i * D : (i + 1) * D].astype(F32), axis=1, keepdims=True)
        d_up[:, i * D : (i + 1) * D] = raw * two
    d_gain_one[...] = as_row(sum_one)
    d_gain_two[...] = as_row(sum_two)


def tables():
    inverse = np.exp(np.arange(64) * (-2.0 * math.log(10000.0) / HEAD_DIM))
    angles = np.arange(GROUP)[:, None] * inverse[None, :]
    return np.concatenate([np.cos(angles), np.sin(angles)], axis=1).astype(np.float32).reshape(4, 2, 128, 128)


def shapes_of(pairs):
    return [jax.ShapeDtypeStruct(s, t) for s, t in pairs]


def per_device(
    block_input, doc_lengths, ffn_levels, attn_gain, qkv_weight, out_weight, ffn_gain, up_weight, down_weight, grad_output
):
    vmem = pl.BlockSpec(memory_space=pltpu.VMEM)
    smem = pl.BlockSpec(memory_space=pltpu.SMEM)
    gain_one, gain_two = attn_gain.reshape(1, 12), ffn_gain.reshape(1, 12)
    outs = [((128, D), BF), ((128, D), F32), ((4, 16, 1152), BF), ((4, 16, D), BF), ((48, D), BF), ((16, D), BF)]
    made = pl.pallas_call(
        layer_kernel,
        out_shape=shapes_of(outs),
        in_specs=[smem] * 2 + [vmem] * 9,
        out_specs=[vmem] * len(outs),
        scratch_shapes=scratch_list(),
        compiler_params=pltpu.CompilerParams(collective_id=0, has_side_effects=True, vmem_limit_bytes=VMEM_LIMIT),
        name="layer_kernel",
    )(
        doc_lengths, ffn_levels, block_input[0], grad_output[0], qkv_weight, out_weight, up_weight, down_weight,
        gain_one, gain_two, jnp.asarray(tables()),
    )
    outs = [((128, D), BF), ((128, D), F32), ((1, 12), F32), ((12, 3 * D), F32), ((12, D), F32), ((1, 12), F32)]
    outs += [((12, FF), F32), ((48, D), F32)]
    block, grad, d_gain_one, d_qkv, d_out, d_gain_two, d_up, d_down = pl.pallas_call(
        finish_kernel,
        out_shape=shapes_of(outs),
        in_specs=[vmem] * 10,
        out_specs=[vmem] * len(outs),
        compiler_params=pltpu.CompilerParams(vmem_limit_bytes=VMEM_LIMIT),
        name="finish_kernel",
    )(*made, qkv_weight, up_weight, gain_one, gain_two)
    return block[None], grad[None], d_gain_one.reshape(12), d_qkv, d_out, d_gain_two.reshape(12), d_up, d_down


def solution(mesh):
    rows = P("batch", "seq", None)
    every = ("batch", "seq")
    return jax.shard_map(
        per_device,
        mesh=mesh,
        in_specs=(rows, P("batch", None), P("batch", None), P(every), P(every, None), P(every, None), P(every),
                  P(every, None), P(every, None), rows),
        out_specs=(rows, rows, P(every), P(every, None), P(every, None), P(every), P(every, None), P(every, None)),
        check_vma=False,
    )
```

```python
import math

import jax
import jax.numpy as jnp
import numpy as np
from jax import lax
from jax.experimental import pallas as pl
from jax.experimental.pallas import tpu as pltpu
from jax.sharding import PartitionSpec as P

HEADS = 12
HEAD_DIM = 128
D = 1536
FF = 6144
DOCS = 6
GROUP = 1024
SHARD = 128
RANK_HEADS = 3
RANK_COLS = 384
EPS = 1e-06
VMEM_LIMIT = 63 * 2**20
BF = jnp.bfloat16
F32 = jnp.float32
MESH = pl.DeviceIdType.MESH


def coords():
    b = lax.axis_index("batch")
    s = lax.axis_index("seq")
    return b // 4, (b // 2) % 2, b % 2, s // 2, s % 2


def dev(y, zl, c, x, zh):
    return (y * 4 + zl * 2 + c, x * 2 + zh)


def x_peers():
    y, zl, c, x, zh = coords()
    return [dev(y, zl, c, (x + k) % 4, zh) for k in (1, 2, 3)]


def y_peers():
    y, zl, c, x, zh = coords()
    return [dev((y + k) % 4, zl, c, x, zh) for k in (1, 2, 3)]


def z_peers():
    y, zl, c, x, zh = coords()
    z = zh * 2 + zl
    return [dev(y, (z + k) % 2, c, x, ((z + k) % 4) // 2) for k in (1, 2, 3)]


def core_peer():
    y, zl, c, x, zh = coords()
    return dev(y, zl, 1 - c, x, zh)


def zh_peer():
    y, zl, c, x, zh = coords()
    return dev(y, zl, c, x, 1 - zh)


class Lines:
    def __init__(self, send, recv):
        self.send, self.recv, self.used = send, recv, 0

    def copy(self, src, dst, peer):
        at = self.used
        self.used += 1
        return pltpu.make_async_remote_copy(
            src, dst, self.send.at[at], self.recv.at[at], device_id=peer, device_id_type=MESH
        )


LO, HI = pl.ds(0, 64), pl.ds(64, 64)


def ring(axis):
    y, zl, c, x, zh = coords()
    if axis == "x":
        return x, x_peers()[0], x_peers()[2]
    if axis == "y":
        return y, y_peers()[0], y_peers()[2]
    return zh * 2 + zl, z_peers()[0], z_peers()[2]


class RingGather:
    def __init__(self, lines, axis, lo, hi):
        self.lines, self.axis, self.lo, self.hi = lines, axis, lo, hi

    def start(self):
        me, nxt, prv = ring(self.axis)
        lo, hi = self.lo(me), self.hi(me)
        self.first = self.lines.copy(lo, lo, nxt)
        self.second = self.lines.copy(hi, hi, prv)
        self.rest = [self.lines.copy(hi, hi, nxt), self.lines.copy(lo, lo, prv)]
        for cp in (self.first, self.second, *self.rest):
            cp.start()

    def on(self):
        me, nxt, prv = ring(self.axis)
        lo, hi = self.lo((me + 3) % 4), self.hi((me + 1) % 4)
        self.first.wait_recv()
        one = self.lines.copy(lo, lo, nxt)
        one.start()
        self.second.wait_recv()
        two = self.lines.copy(hi, hi, prv)
        two.start()
        self.rest += [one, two]

    def near(self):
        for cp in self.rest[:2]:
            cp.wait()
        self.rest = self.rest[2:]

    def finish(self):
        self.first.wait_send()
        self.second.wait_send()
        for cp in self.rest:
            cp.wait()


class RingScatter:
    def __init__(self, lines, axis, lo, hi, got, via):
        self.lines, self.axis, self.lo, self.hi, self.got, self.via = lines, axis, lo, hi, got, via

    def start(self):
        self.start_far()
        self.start_near()

    def start_far(self):
        me, nxt, prv = ring(self.axis)
        far = (me + 2) % 4
        self.far_lo = self.lines.copy(self.lo(far), self.via.at[0], nxt)
        self.far_hi = self.lines.copy(self.hi(far), self.via.at[1], prv)
        self.far_lo.start()
        self.far_hi.start()

    def start_near(self):
        me, nxt, prv = ring(self.axis)
        left, right = (me + 3) % 4, (me + 1) % 4
        self.rest = [
            self.lines.copy(self.hi(right), self.got.at[2], nxt),
            self.lines.copy(self.lo(left), self.got.at[0], prv),
        ]
        for cp in self.rest:
            cp.start()

    def on(self):
        me, nxt, prv = ring(self.axis)
        left, right = (me + 3) % 4, (me + 1) % 4
        via = self.via
        self.far_lo.wait_recv()
        via[0] = (via[0].astype(F32) + self.lo(right)[...].astype(F32)).astype(BF)
        one = self.lines.copy(via.at[0], self.got.at[1], nxt)
        one.start()
        self.far_hi.wait_recv()
        via[1] = (via[1].astype(F32) + self.hi(left)[...].astype(F32)).astype(BF)
        two = self.lines.copy(via.at[1], self.got.at[3], prv)
        two.start()
        self.rest += [one, two]

    def finish(self):
        self.far_lo.wait_send()
        self.far_hi.wait_send()
        for cp in self.rest:
            cp.wait()

    def others(self):
        got = self.got
        return got[0].astype(F32) + got[1].astype(F32), got[2].astype(F32) + got[3].astype(F32)

    def total(self, own):
        return own + jnp.concatenate(self.others(), axis=0)


def gather_x(lines, place):
    return RingGather(lines, "x", lambda i: place(i, LO), lambda i: place(i, HI))


def scatter_x(lines, parts, got, via):
    return RingScatter(lines, "x", lambda i: parts.at[i, LO], lambda i: parts.at[i, HI], got, via)


def one_hot_rows(rows, cols, expand):
    i = lax.broadcasted_iota(jnp.int32, (rows, cols), 0)
    j = lax.broadcasted_iota(jnp.int32, (rows, cols), 1)
    a, p = (j, i) if expand else (i, j)
    return jnp.where((p % 16 < 12) & (p // 16 * 12 + p % 16 == a), 1.0, 0.0).astype(BF)


def pick(matrix, values):
    return jnp.dot(matrix, values, preferred_element_type=F32).astype(BF)


def seq_peers():
    y, zl, c, x, zh = coords()
    s = x * 2 + zh
    found = []
    for k in range(1, 8):
        t = (s + k) % 8
        found.append(dev(y, zl, c, t // 2, t % 2))
    return found


def greet():
    y, _, _, x, _ = coords()
    sem = pltpu.get_barrier_semaphore()
    peers = seq_peers() + y_peers() + z_peers()[::2] + [core_peer()]
    for peer in peers:
        pl.semaphore_signal(sem, inc=1, device_id=peer, device_id_type=MESH)

    @pl.when(x != y)
    def _():
        pl.semaphore_signal(sem, inc=1, device_id=swap_xy(), device_id_type=MESH)

    return len(peers) + jnp.where(x != y, 1, 0)


def swap_xy():
    y, zl, c, x, zh = coords()
    return dev(x, zl, c, y, zh)


def spread(lines, src, dst):
    y, zl, c, x, zh = coords()
    s = x * 2 + zh
    at = lines.used
    lines.used += 4
    sends, arrivals = [], []
    for k in range(4):
        i = (x + k) % 4
        own = (i == x) & (x // 2 == zh)
        cp = pltpu.make_async_remote_copy(
            src.at[i], dst.at[s % 4], lines.send.at[at + k], lines.recv.at[at + s % 4],
            device_id=dev(y, zl, c, i, x // 2), device_id_type=MESH,
        )
        sends.append((cp, own))
    for j in range(4):
        own = (x // 2 == zh) & (s % 4 == j)
        cp = pltpu.make_async_remote_copy(
            src.at[j], dst.at[j], lines.send.at[at], lines.recv.at[at + j],
            device_id=core_peer(), device_id_type=MESH,
        )
        arrivals.append((cp, own))
    return sends, arrivals, (x // 2 == zh), x, s % 4


def gather_home(lines, src, dst):
    y, zl, c, x, zh = coords()
    s = x * 2 + zh
    at = lines.used
    lines.used += 4
    sends, arrivals = [], []
    for k in range(4):
        i = (s + k) % 4
        t = 4 * zh + i
        own = t == s
        cp = pltpu.make_async_remote_copy(
            src.at[i], dst.at[x], lines.send.at[at + k], lines.recv.at[at + x],
            device_id=dev(y, zl, c, t // 2, t % 2), device_id_type=MESH,
        )
        sends.append((cp, own))
    for j in range(4):
        own = (x // 2 == zh) & (x == j)
        cp = pltpu.make_async_remote_copy(
            src.at[j], dst.at[j], lines.send.at[at], lines.recv.at[at + j],
            device_id=core_peer(), device_id_type=MESH,
        )
        arrivals.append((cp, own))
    return sends, arrivals, (x // 2 == zh), s % 4, x


def start_all(plan, src, dst):
    sends, _, mine, from_slot, to_slot = plan
    for cp, own in sends:
        pl.when(jnp.logical_not(own))(cp.start)

    @pl.when(mine)
    def _():
        dst[to_slot] = src[from_slot]


def wait_all(plan):
    sends, arrivals = plan[:2]
    for cp, own in arrivals:
        pl.when(jnp.logical_not(own))(cp.wait_recv)
    for cp, own in sends:
        pl.when(jnp.logical_not(own))(cp.wait_send)


class Gather:
    def __init__(self, lines, full, rows, z_first, y_inner=False, columns=None):
        self.lines, self.full, self.rows, self.z_first, self.y_inner = lines, full, rows, z_first, y_inner
        self.columns = pl.ds(0, full.shape[-1]) if columns is None else columns
        self.pending = []

    def _at(self, y, zl, c, rows):
        place = (zl, c, y) if self.y_inner else (y, zl, c)
        return self.full.at[(*place, rows, self.columns)]

    def _send(self, src, peers):
        copies = [self.lines.copy(src, src, p) for p in peers]
        for cp in copies:
            cp.start()
        self.pending = copies

    def near(self):
        y, zl, c, _, zh = coords()
        mine = self._at(y, zl, c, pl.ds(zh * self.rows, self.rows))
        self._send(mine, z_peers() if self.z_first else y_peers())

    def wide(self):
        self.wait()
        y, zl, c, _, zh = coords()
        if self.z_first:
            rows = pl.ds(0, 2 * self.rows)
            self.ring = RingGather(
                self.lines, "y", lambda i: self._at(i, 0, c, rows), lambda i: self._at(i, 1, c, rows)
            )
        else:
            rows = lambda i: pl.ds(i // 2 * self.rows, self.rows)
            self.ring = RingGather(
                self.lines, "z", lambda i: self._at(pl.ds(0, 2), i % 2, c, rows(i)),
                lambda i: self._at(pl.ds(2, 2), i % 2, c, rows(i)),
            )
        self.ring.start()

    def on(self):
        self.ring.on()

    def cores(self):
        self.ring.finish()
        c = coords()[2]
        self._send(self._at(slice(None), slice(None), c, pl.ds(0, 2 * self.rows)), [core_peer()])

    def wait(self):
        for cp in self.pending:
            cp.wait()
        self.pending = []


class Scatter:
    def __init__(self, lines, part, bufs, rows, y_first, y_inner=False, columns=None):
        self.lines, self.part = lines, part
        self.half, self.got, self.via, self.wide, self.wide_in = bufs
        self.rows, self.y_first, self.y_inner, self.pending = rows, y_first, y_inner, []
        self.columns = pl.ds(0, part.shape[-1]) if columns is None else columns

    def wait(self):
        for cp in self.pending:
            cp.wait()
        self.pending = []

    def _start(self, copies):
        for cp in copies:
            cp.start()
        self.pending = copies

    def cores(self):
        c = coords()[2]
        rows = pl.ds(0, 2 * self.rows)
        place = (slice(None), 1 - c, slice(None)) if self.y_inner else (slice(None), slice(None), 1 - c)
        self._start([self.lines.copy(self.part.at[(*place, rows, self.columns)], self.half, core_peer())])

    def _block(self, side, i):
        if not self.y_first:
            rows, pair = pl.ds(i // 2 * self.rows, self.rows), pl.ds(2 * side, 2)
            return self.half.at[i % 2, pair, rows] if self.y_inner else self.half.at[pair, i % 2, rows]
        return self.half.at[side, i] if self.y_inner else self.half.at[i, side]

    def first(self):
        self.wait()
        c, inner = coords()[2], self.half.shape[1]

        @pl.loop(0, 8)
        def _(i):
            a, b = i // inner, i % inner
            place = (a, c, b) if self.y_inner else (a, b, c)
            both = self.part[(*place, slice(None), self.columns)].astype(F32) + self.half[a, b].astype(F32)
            self.half[a, b] = both.astype(BF)

        self.ring = RingScatter(
            self.lines, "y" if self.y_first else "z", lambda i: self._block(0, i), lambda i: self._block(1, i),
            self.got, self.via,
        )
        self.ring.start()

    def on(self):
        self.ring.on()

    def second(self):
        self.ring.finish()
        me = ring("y" if self.y_first else "z")[0]
        for side, others in enumerate(self.ring.others()):
            self.wide[side] = (self._block(side, me)[...].astype(F32) + others).astype(BF)
        copies = []
        for k in (1, 2, 3):
            peer = (z_peers if self.y_first else y_peers)()[k - 1]
            copies.append(self.lines.copy(self._piece(k), self.wide_in.at[k - 1], peer))
        self._start(copies)

    def _piece(self, k):
        y, zl, c, _, zh = coords()
        if self.y_first:
            zz = (zh * 2 + zl + k) % 4
            return self.wide.at[zz % 2, pl.ds(zz // 2 * self.rows, self.rows)]
        yy = (y + k) % 4
        return self.wide.at[yy // 2, yy % 2]

    def total(self):
        self.wait()
        total = self._piece(0)[...].astype(F32)
        for k in range(3):
            total += self.wide_in[k].astype(F32)
        return total


class Pair:
    def __init__(self, *parts):
        self.parts = parts

    def __getattr__(self, step):
        return lambda: [getattr(p, step)() for p in self.parts]

    def sums(self):
        return jnp.concatenate([p.total().astype(BF) for p in self.parts], axis=1)


def gather_both(lines, full, rows, split, width, y_inner=False):
    return Pair(
        Gather(lines, full, rows, True, y_inner, pl.ds(0, split)),
        Gather(lines, full, rows, False, y_inner, pl.ds(split, width - split)),
    )


def scatter_both(lines, part, bufs, rows, split, width, y_inner=False):
    n = len(bufs) // 2
    return Pair(
        Scatter(lines, part, bufs[:n], rows, False, y_inner, pl.ds(0, split)),
        Scatter(lines, part, bufs[n:], rows, True, y_inner, pl.ds(split, width - split)),
    )


def scatter_scratch(rows, split, width, y_inner=False):
    found = []
    for n, y_first in ((split, False), (width - split, True)):
        half = (2, 4, 2 * rows, n) if y_inner else (4, 2, 2 * rows, n)
        block = (2 * rows, n) if y_first else (2, rows, n)
        found += [pltpu.VMEM(s, BF) for s in (half, (4, *block), (2, *block), (2, *block), (3, rows, n))]
    return found


def dot(a, b):
    return jnp.dot(a, b, preferred_element_type=F32)


def dot_nt(a, b):
    return lax.dot_general(a, b, (((1,), (1,)), ((), ())), preferred_element_type=F32)


def dot_tn(a, b):
    return lax.dot_general(a, b, (((0,), (0,)), ((), ())), preferred_element_type=F32)


def normalize(values):
    r = lax.rsqrt(jnp.mean(values * values, axis=-1, keepdims=True) + EPS)
    return r, values * r


def rms_back(grad, values):
    r, hat = normalize(values)
    return r * (grad - hat * jnp.mean(grad * hat, axis=-1, keepdims=True))


def cos_sin(table):
    other = pltpu.roll(table, 64, 1)
    low = lax.broadcasted_iota(jnp.int32, table.shape, 1) < 64
    return jnp.where(low, table, other), jnp.where(low, -other, table)


def turn(v, cos, sin):
    return v * cos + pltpu.roll(v, 64, 1) * sin


def turn_back(v, cos, sin):
    return v * cos - pltpu.roll(v, 64, 1) * sin


GELU_A, GELU_B = math.sqrt(2.0 / math.pi), 0.044715


def gelu_both(v):
    square = v * v
    t = jnp.tanh(GELU_A * v * (1.0 + GELU_B * square))
    half = 0.5 * (1.0 + t)
    return v * half, half + 0.5 * v * (1.0 - t * t) * (GELU_A * (1.0 + 3.0 * GELU_B * square))


def cols(i, n):
    return pl.ds(pl.multiple_of(i * n, n), n)


NAMES = (
    "full_q", "full_u", "full_d", "full_o", "got_q", "got_u", "src_q", "src_u", "src_o",
    "normed", "q_ref", "k_ref", "v_ref", "p0", "p1", "p2", "p3",
    "att", "att_grad", "middle", "wo", "ntwo", "up_grad", "hidden", "pre_grad", "branch", "part_a",
    "got_a", "via_a", "got_b", "via_b", "swap_in", "dk_t", "dv_t",
    *(f"s{w}{k}" for w in "qudo" for k in range(10)), "send", "recv",
    "tokens", "qkv", "grad_in", "up", "out_w", "down", "angles", "load",
)


def scratch_list():
    V = pltpu.VMEM
    block = V((4, 128, D), BF)
    got, via = V((4, 64, D), BF), V((2, 64, D), BF)
    kv = V((3, 4, 2, 128, 128), BF)
    shapes = [V((4, 2, 2, 96, 1152), BF), V((4, 2, 2, 96, D), BF), V((2, 2, 4, 96, D), BF), V((2, 2, 4, 32, D), BF)]
    shapes += [V((4, 16, 1152), BF), V((4, 16, D), BF)] * 2 + [V((16, D), BF)]
    shapes += [V((4, 2, 128, D), BF), V((3, 4, 128, 128), BF), kv, kv]
    shapes += [V((3, 128, 256 * (i + 1)), BF) for i in range(4)]
    shapes += [V((4, 128, RANK_COLS), BF), V((4, 128, RANK_COLS), BF), V((128, D), F32), V((RANK_COLS, D), BF)]
    shapes += [block] * 6
    shapes += [got, via] * 2 + [V((128, D), BF)]
    shapes += [V((128, GROUP), F32), V((128, GROUP), F32)]
    shapes += scatter_scratch(48, RANK_COLS, 1152) + scatter_scratch(48, 768, D)
    shapes += scatter_scratch(48, 768, D, True) + scatter_scratch(16, 768, D, True)
    shapes += [pltpu.SemaphoreType.DMA((300,)), pltpu.SemaphoreType.DMA((300,))]
    rows = V((128, D), BF)
    shapes += [rows, V((12, 3 * D), BF), rows, V((12, FF), BF), V((12, D), BF), V((48, D), BF)]
    shapes += [V((4, 2, 128, 128), F32), pltpu.SemaphoreType.DMA((7,))]
    assert len(shapes) == len(NAMES)
    return shapes


class Refs:
    pass


def column(row):
    n = row.shape[1]
    same = lax.broadcasted_iota(jnp.int32, (n, n), 0) == lax.broadcasted_iota(jnp.int32, (n, n), 1)
    return jnp.sum(jnp.where(same, row, 0.0), axis=1, keepdims=True)


def as_row(col):
    n = col.shape[0]
    same = lax.broadcasted_iota(jnp.int32, (n, n), 0) == lax.broadcasted_iota(jnp.int32, (n, n), 1)
    return jnp.sum(jnp.where(same, col, 0.0), axis=0, keepdims=True)


def sixteen(rows):
    return jnp.concatenate([rows, jnp.zeros((4, rows.shape[1]), rows.dtype)], axis=0).astype(BF)


def documents(lengths, levels, positions):
    start, width = jnp.zeros_like(positions), jnp.zeros_like(positions)
    first = 0
    for d in range(DOCS):
        level = levels[0, d]
        wide = jnp.where(level == 0, FF // 8, jnp.where(level == 1, FF // 4, jnp.where(level == 2, FF // 2, FF)))
        inside = positions >= first
        start = jnp.where(inside, first, start)
        width = jnp.where(inside, wide, width)
        first = first + lengths[0, d]
    return start, width


def layer_kernel(
    lengths, levels, gain_one, gain_two, tokens_in, grad_in_in, qkv_in, out_w_in, up_in, down_in, angles_in,
    block_out, grad_input, out_q, out_u, out_d, out_o, *scratch
):
    g = Refs()
    for name, ref in zip(NAMES, scratch):
        setattr(g, name, ref)
    bufs = lambda w: [getattr(g, f"s{w}{k}") for k in range(10)]
    y, zl, c, x, zh = coords()
    lines = Lines(g.send, g.recv)
    scale = HEAD_DIM**-0.5
    greetings = greet()

    tokens, grad_in, qkv, out_w, up, down, angles = g.tokens, g.grad_in, g.qkv, g.out_w, g.up, g.down, g.angles
    pairs = [
        (tokens_in, tokens), (qkv_in, qkv), (grad_in_in, grad_in), (up_in, up), (out_w_in, out_w), (down_in, down),
        (angles_in, angles),
    ]
    loads = [pltpu.make_async_copy(a, b, g.load.at[k]) for k, (a, b) in enumerate(pairs)]
    for cp in loads:
        cp.start()
    loads[0].wait()
    g.normed[x, zh] = normalize(tokens[...].astype(F32))[1].astype(BF)
    one, two = column(gain_one[...].astype(F32)), column(gain_two[...].astype(F32))
    loads[1].wait()
    for i in range(4):
        for j in range(3):
            at = j * D + i * RANK_COLS
            g.src_q[i, :, j * RANK_COLS : (j + 1) * RANK_COLS] = sixteen(qkv[:, at : at + RANK_COLS].astype(F32) * one)
    for cp in loads[2:5]:
        cp.wait()
    g.up_grad[x] = grad_in[...]
    for i in range(4):
        g.src_u[i] = sixteen(up[:, i * D : (i + 1) * D].astype(F32) * two)
    g.src_o[...] = sixteen(out_w[...].astype(F32))
    for cp in loads[5:]:
        cp.wait()
    pl.semaphore_wait(pltpu.get_barrier_semaphore(), greetings)

    ring_one = gather_x(lines, lambda i, h: g.normed.at[i, zh, h])
    ring_two = gather_x(lines, lambda i, h: g.normed.at[i, 1 - zh, h])
    swap = lines.copy(g.normed.at[x, zh], g.normed.at[x, zh], zh_peer())
    plan_q = spread(lines, g.src_q, g.got_q)
    start_all(plan_q, g.src_q, g.got_q)
    swap_o = lines.copy(g.src_o, g.full_o.at[zl, c, x, pl.ds(zh * 16, 16)], swap_xy())
    swap_d = lines.copy(down, g.full_d.at[zl, c, x, pl.ds(zh * 48, 48)], swap_xy())
    swap.start()
    ring_one.start()
    pl.when(x != y)(swap_o.start)
    rows = one_hot_rows(48, 64, False)
    wait_all(plan_q)
    g.full_q[y, zl, c, pl.ds(zh * 48, 48)] = pick(rows, g.got_q[...].reshape(64, 1152))
    gather_q = gather_both(lines, g.full_q, 48, 256, 1152)
    gather_o = Gather(lines, g.full_o, 16, True, True)
    gather_u = gather_both(lines, g.full_u, 48, 768, D)
    gather_d = gather_both(lines, g.full_d, 48, 768, D, True)
    gather_q.near()

    @pl.when(x == y)
    def _():
        g.full_o[zl, c, x, pl.ds(zh * 16, 16)] = g.src_o[...]
        g.full_d[zl, c, x, pl.ds(zh * 48, 48)] = down[...]

    ring_one.on()
    gather_q.wide()
    pl.when(x != y)(swap_d.start)
    swap.wait_recv()
    ring_two.start()
    gather_q.on()
    pl.when(x != y)(swap_o.wait)
    gather_o.near()
    plan_u = spread(lines, g.src_u, g.got_u)
    start_all(plan_u, g.src_u, g.got_u)
    ring_two.on()
    gather_q.cores()
    gather_o.wide()
    pl.when(x != y)(swap_d.wait)
    gather_d.near()
    ring_one.finish()
    gather_q.wait()

    def project(zz, own_half):
        block = g.normed[:, zz].reshape(512, D)
        cos_b, sin_b = cos_sin(angles[:, zz].reshape(512, 128))
        for j in range(0 if own_half else 1, 3):
            made = dot(block, g.full_q[:, :, :, :, j * RANK_COLS : (j + 1) * RANK_COLS].reshape(D, RANK_COLS))
            for h in range(RANK_HEADS):
                head = made[:, h * 128 : (h + 1) * 128]
                if j < 2:
                    head = turn(head, cos_b, sin_b)
                head = head.astype(BF).reshape(4, 128, 128)
                if j == 0:
                    g.q_ref[h] = head
                elif j == 1:
                    g.k_ref[h, :, zz] = head
                else:
                    g.v_ref[h, :, zz] = head

    project(zh, True)
    gather_o.on()
    gather_d.wide()
    wait_all(plan_u)
    g.full_u[y, zl, c, pl.ds(zh * 48, 48)] = pick(rows, g.got_u[...].reshape(64, D))
    gather_u.near()
    ring_two.finish()
    swap.wait_send()
    ring_up = gather_x(lines, lambda i, h: g.up_grad.at[i, h])
    ring_up.start()
    project(1 - zh, False)
    gather_o.cores()

    probs = [g.p0, g.p1, g.p2, g.p3]

    def attend(h):
        for i in range(4):
            n = 256 * (i + 1)
            keys = g.k_ref[h, : i + 1].reshape(n, 128)
            values = g.v_ref[h, : i + 1].reshape(n, 128)
            scores = dot_nt(g.q_ref[h, i], keys) * scale
            base = (2 * i + zh) * 128
            q_at = base + lax.broadcasted_iota(jnp.int32, (128, n), 0)
            k_at = lax.broadcasted_iota(jnp.int32, (128, n), 1)
            first = documents(lengths, levels, base + lax.broadcasted_iota(jnp.int32, (128, 1), 0))[0]
            scores = jnp.where((k_at <= q_at) & (k_at >= first), scores, -1e30)
            e = jnp.exp(scores - jnp.max(scores, axis=-1, keepdims=True))
            p = (e * (1.0 / jnp.sum(e, axis=-1, keepdims=True))).astype(BF)
            probs[i][h] = p
            g.att[i, :, pl.ds(pl.multiple_of(h * 128, 128), 128)] = dot(p, values).astype(BF)

    attend(0)
    gather_d.on()
    ring_up.on()
    pl.loop(1, RANK_HEADS)(attend)
    gather_o.wait()
    g.wo[...] = pick(one_hot_rows(RANK_COLS, 512, False), g.full_o[...].reshape(512, D))

    def to_parts(parts, left, right_of, transposed, tiles):
        n = D // tiles

        @pl.loop(0, tiles)
        def _(t):
            right = right_of(t)
            made = dot_nt(left(), right) if transposed else dot(left(), right)
            parts[:, :, cols(t, n)] = made.astype(BF).reshape(4, 128, n)

    to_parts(g.part_a, lambda: g.att[...].reshape(512, RANK_COLS), lambda t: g.wo[:, cols(t, 512)], False, 3)
    ring_a = scatter_x(lines, g.part_a, g.got_a, g.via_a)
    ring_a.start()
    gather_u.wide()
    gather_d.cores()

    gather_u.on()
    ring_up.finish()
    gather_d.wait()
    ring_a.on()
    up_all = lambda: g.up_grad[...].reshape(512, D)
    to_parts(g.pre_grad, up_all, lambda t: g.full_d[t].reshape(768, D), True, 2)
    gather_u.cores()
    ring_a.finish()
    g.middle[...] = ring_a.total(tokens[...].astype(F32) + g.part_a[x].astype(F32))
    g.ntwo[x] = normalize(g.middle[...])[1].astype(BF)
    ring_n = gather_x(lines, lambda i, h: g.ntwo.at[i, h])
    ring_n.start()

    def full_rows(ref, t):
        return ref[pl.ds(t * 2, 2)].reshape(768, ref.shape[-1])

    def full_cols(ref, t, n):
        return ref[:, :, :, :, cols(t, n)].reshape(D, n)

    gather_u.wait()

    def feed_forward(blocks, tile):
        rows = 128 * len(blocks)
        at = [(2 * i + zh) * 128 + lax.broadcasted_iota(jnp.int32, (128, 1), 0) for i in blocks]
        width = jnp.concatenate([documents(lengths, levels, p)[1] for p in at], axis=0)

        @pl.loop(0, D // tile)
        def _(t):
            normed_rows = jnp.concatenate([g.ntwo[i] for i in blocks], axis=0)
            pre = dot(normed_rows, full_cols(g.full_u, t, tile))
            unit = x * D + t * tile + lax.broadcasted_iota(jnp.int32, (rows, tile), 1)
            mask = unit < width
            act, slope = gelu_both(pre)
            act = jnp.where(mask, act, 0.0).astype(BF)
            slope = jnp.where(mask, slope, 0.0)
            for k, i in enumerate(blocks):
                own = slice(128 * k, 128 * (k + 1))
                g.hidden[i, :, cols(t, tile)] = act[own]
                back = g.pre_grad[i, :, cols(t, tile)].astype(F32)
                g.pre_grad[i, :, cols(t, tile)] = (slope[own] * back).astype(BF)

        @pl.loop(0, 2)
        def _(t):
            pre_rows = jnp.concatenate([g.pre_grad[i] for i in blocks], axis=0)
            made = dot_nt(pre_rows, full_rows(g.full_u, t)).astype(BF)
            for k, i in enumerate(blocks):
                g.part_a[i, :, cols(t, 768)] = made[128 * k : 128 * (k + 1)]

    feed_forward([x], 512)
    ring_n.on()
    ring_n.near()
    ring_b = scatter_x(lines, g.part_a, g.got_b, g.via_b)
    feed_forward([(x + 3) % 4, (x + 1) % 4], 256)
    ring_b.start_near()
    ring_n.finish()
    feed_forward([(x + 2) % 4], 512)
    ring_b.start_far()
    pre_all = lambda: g.pre_grad[...].reshape(512, D)

    def weight_grad(full, left_of, right):
        @pl.loop(0, 4)
        def _(t):
            made = dot_tn(left_of(t), right()).astype(BF)
            if full.shape[0] == 4:
                full[t] = made.reshape(full.shape[1:])
            else:
                full[t // 2, t % 2] = made.reshape(full.shape[2:])

    weight_grad(g.full_u, lambda t: g.ntwo[:, :, cols(t, 384)].reshape(512, 384), pre_all)
    scatter_u = scatter_both(lines, g.full_u, bufs("u"), 48, 768, D)
    scatter_u.cores()
    ring_b.on()
    to_parts(g.pre_grad, lambda: g.hidden[...].reshape(512, D), lambda t: full_cols(g.full_d, t, 512), False, 3)
    scatter_u.first()
    ring_b.finish()

    grad_input[...] = grad_in[...].astype(F32) + rms_back(ring_b.total(g.part_a[x].astype(F32)), g.middle[...])
    g.branch[x] = grad_input[...].astype(BF)
    ring_g = gather_x(lines, lambda i, h: g.branch.at[i, h])
    ring_g.start()
    weight_grad(g.full_d, lambda t: g.hidden[:, :, cols(t, 384)].reshape(512, 384), up_all)
    scatter_d = scatter_both(lines, g.full_d, bufs("d"), 48, 768, D, True)
    scatter_d.cores()
    padded = pick(g.att[...].reshape(512, RANK_COLS), one_hot_rows(RANK_COLS, 512, False))
    g.hidden[:, :, :512] = padded.reshape(4, 128, 512)
    scatter_u.on()
    ring_g.on()
    scatter_d.first()
    ring_g.finish()
    ring_c = scatter_x(lines, g.pre_grad, g.up_grad.at[:, LO], g.up_grad.at[pl.ds(0, 2), HI])
    ring_c.start()

    branch_all = lambda: g.branch[...].reshape(512, D)
    scatter_u.second()
    g.att_grad[...] = dot_nt(branch_all(), g.wo[...]).astype(BF).reshape(4, 128, RANK_COLS)

    def attend_back(h):
        at = pl.ds(pl.multiple_of(h * 128, 128), 128)
        g.dk_t[...] = jnp.zeros_like(g.dk_t)
        g.dv_t[...] = jnp.zeros_like(g.dv_t)
        for i in range(4):
            n = 256 * (i + 1)
            keys = g.k_ref[h, : i + 1].reshape(n, 128)
            values = g.v_ref[h, : i + 1].reshape(n, 128)
            queries = g.q_ref[h, i]
            p = probs[i][h]
            grad = g.att_grad[i, :, at]
            delta = jnp.sum(grad.astype(F32) * g.att[i, :, at].astype(F32), axis=-1, keepdims=True)
            ds = (p.astype(F32) * (dot_nt(grad, values) - delta)).astype(BF)
            dq = dot(ds, keys) * scale
            g.dk_t[:, :n] += dot(queries.T, ds)
            g.dv_t[:, :n] += dot(grad.T, p)
            g.q_ref[h, i] = turn_back(dq, *cos_sin(angles[i, zh])).astype(BF)
        dk = g.dk_t[...].T * scale
        dk = turn_back(dk, *cos_sin(angles[...].reshape(GROUP, 128)))
        g.k_ref[h] = dk.astype(BF).reshape(4, 2, 128, 128)
        g.v_ref[h] = g.dv_t[...].T.astype(BF).reshape(4, 2, 128, 128)

    attend_back(0)
    scatter_d.on()
    pl.loop(1, RANK_HEADS)(attend_back)
    ring_c.on()

    def side(ref, zz):
        return [ref[h, :, zz].reshape(512, 128) for h in range(RANK_HEADS)]

    def first_parts(parts, zz, own_half):
        def left():
            pieces = side(g.k_ref, zz) + side(g.v_ref, zz)
            if own_half:
                pieces = [g.q_ref[h].reshape(512, 128) for h in range(RANK_HEADS)] + pieces
            return jnp.concatenate(pieces, axis=1)

        n = 1152 if own_half else 768
        to_parts(parts, left, lambda t: g.full_q[pl.ds(t * 2, 2), :, :, :, 1152 - n :].reshape(768, n), True, 2)

    first_parts(g.part_a, 1 - zh, False)
    ring_e = scatter_x(lines, g.part_a, g.got_a, g.via_a)
    ring_e.start()
    weight_grad(g.full_o, lambda t: g.hidden[:, :, cols(t, 128)].reshape(512, 128), branch_all)
    scatter_o = scatter_both(lines, g.full_o, bufs("o"), 16, 768, D, True)
    scatter_o.cores()
    scatter_q = scatter_both(lines, g.full_u, bufs("q"), 48, RANK_COLS, 1152)
    part_q, part_kv = scatter_q.parts
    dq_all = lambda: jnp.concatenate([g.q_ref[h].reshape(512, 128) for h in range(RANK_HEADS)], axis=1)
    dkv_all = lambda: jnp.concatenate(
        [r[h].reshape(GROUP, 128) for r in (g.k_ref, g.v_ref) for h in range(RANK_HEADS)], axis=1
    )

    @pl.loop(0, 4)
    def _(t):
        every = g.normed[:, :, :, cols(t, 384)].reshape(GROUP, 384)
        g.full_u[t, :, :, :, RANK_COLS:1152] = dot_tn(every, dkv_all()).astype(BF).reshape(2, 2, 96, 768)

    part_kv.cores()
    scatter_o.first()
    scatter_d.second()
    spread_rows = one_hot_rows(64, 48, True)
    g.got_u[...] = pick(spread_rows, scatter_u.sums()).reshape(4, 16, D)
    plan_u = gather_home(lines, g.got_u, out_u)
    start_all(plan_u, g.got_u, out_u)

    @pl.loop(0, 4)
    def _(t):
        mine = g.normed[:, zh, :, cols(t, 384)].reshape(512, 384)
        g.full_u[t, :, :, :, :RANK_COLS] = dot_tn(mine, dq_all()).astype(BF).reshape(2, 2, 96, RANK_COLS)

    part_q.cores()
    part_kv.first()
    ring_e.on()
    part_q.first()
    first_parts(g.ntwo, zh, True)
    ring_f = scatter_x(lines, g.ntwo, g.got_b, g.via_b)
    ring_f.start()
    scatter_o.on()
    scatter_q.on()
    scatter_o.second()
    g.down[...] = scatter_d.sums()
    home_d = lines.copy(g.down, out_d, swap_xy())
    home_o = lines.copy(g.src_o, out_o, swap_xy())
    pl.when(x != y)(home_d.start)
    ring_e.finish()
    g.grad_in[...] = ring_e.total(g.part_a[x].astype(F32)).astype(BF)
    scatter_q.second()
    back = lines.copy(g.grad_in, g.swap_in, zh_peer())
    back.start()
    ring_f.on()
    ring_c.finish()
    block_out[...] = ring_c.total(g.middle[...] + g.pre_grad[x].astype(F32)).astype(BF)
    g.src_o[...] = scatter_o.sums()
    pl.when(x != y)(home_o.start)

    g.got_q[...] = pick(spread_rows, scatter_q.sums()).reshape(4, 16, 1152)
    plan_q = gather_home(lines, g.got_q, out_q)
    start_all(plan_q, g.got_q, out_q)
    ring_f.finish()
    back.wait()
    h_one = ring_f.total(g.ntwo[x].astype(F32)) + g.swap_in[...].astype(F32)
    grad_input[...] += rms_back(h_one, tokens[...].astype(F32))

    @pl.when(x == y)
    def _():
        out_o[...] = g.src_o[...]
        out_d[...] = g.down[...]

    wait_all(plan_u)

    @pl.when(x != y)
    def _():
        home_d.wait()
        home_o.wait()

    wait_all(plan_q)


def finish_kernel(
    block, grad, got_q, got_u, got_d, got_o, qkv, up, gain_one, gain_two,
    block_out, grad_input, d_gain_one, d_qkv, d_out, d_gain_two, d_up, d_down
):
    block_out[...] = block[...]
    grad_input[...] = grad[...]
    d_down[...] = got_d[...].astype(F32)
    d_out[...] = got_o[:12].astype(F32)
    one, two = column(gain_one[...].astype(F32)), column(gain_two[...].astype(F32))
    sum_one = sum_two = jnp.zeros((12, 1), F32)
    for i in range(4):
        for j in range(3):
            raw = got_q[i, :12, j * RANK_COLS : (j + 1) * RANK_COLS].astype(F32)
            at = j * D + i * RANK_COLS
            sum_one += jnp.sum(raw * qkv[:, at : at + RANK_COLS].astype(F32), axis=1, keepdims=True)
            d_qkv[:, at : at + RANK_COLS] = raw * one
        raw = got_u[i, :12].astype(F32)
        sum_two += jnp.sum(raw * up[:, i * D : (i + 1) * D].astype(F32), axis=1, keepdims=True)
        d_up[:, i * D : (i + 1) * D] = raw * two
    d_gain_one[...] = as_row(sum_one)
    d_gain_two[...] = as_row(sum_two)


def tables():
    inverse = np.exp(np.arange(64) * (-2.0 * math.log(10000.0) / HEAD_DIM))
    angles = np.arange(GROUP)[:, None] * inverse[None, :]
    return np.concatenate([np.cos(angles), np.sin(angles)], axis=1).astype(np.float32).reshape(4, 2, 128, 128)


def shapes_of(pairs):
    return [jax.ShapeDtypeStruct(s, t) for s, t in pairs]


def per_device(
    block_input, doc_lengths, ffn_levels, attn_gain, qkv_weight, out_weight, ffn_gain, up_weight, down_weight, grad_output
):
    vmem = pl.BlockSpec(memory_space=pltpu.VMEM)
    smem = pl.BlockSpec(memory_space=pltpu.SMEM)
    gain_one, gain_two = attn_gain.reshape(1, 12), ffn_gain.reshape(1, 12)
    outs = [((128, D), BF), ((128, D), F32), ((4, 16, 1152), BF), ((4, 16, D), BF), ((48, D), BF), ((16, D), BF)]
    made = pl.pallas_call(
        layer_kernel,
        out_shape=shapes_of(outs),
        in_specs=[smem] * 2 + [vmem] * 2 + [pl.BlockSpec(memory_space=pl.ANY)] * 7,
        out_specs=[vmem] * len(outs),
        scratch_shapes=scratch_list(),
        compiler_params=pltpu.CompilerParams(collective_id=0, has_side_effects=True, vmem_limit_bytes=VMEM_LIMIT),
        name="layer_kernel",
    )(
        doc_lengths, ffn_levels, gain_one, gain_two, block_input[0], grad_output[0], qkv_weight, out_weight, up_weight,
        down_weight, jnp.asarray(tables()),
    )
    outs = [((128, D), BF), ((128, D), F32), ((1, 12), F32), ((12, 3 * D), F32), ((12, D), F32), ((1, 12), F32)]
    outs += [((12, FF), F32), ((48, D), F32)]
    block, grad, d_gain_one, d_qkv, d_out, d_gain_two, d_up, d_down = pl.pallas_call(
        finish_kernel,
        out_shape=shapes_of(outs),
        in_specs=[vmem] * 10,
        out_specs=[vmem] * len(outs),
        compiler_params=pltpu.CompilerParams(vmem_limit_bytes=VMEM_LIMIT),
        name="finish_kernel",
    )(*made, qkv_weight, up_weight, gain_one, gain_two)
    return block[None], grad[None], d_gain_one.reshape(12), d_qkv, d_out, d_gain_two.reshape(12), d_up, d_down


def solution(mesh):
    rows = P("batch", "seq", None)
    every = ("batch", "seq")
    return jax.shard_map(
        per_device,
        mesh=mesh,
        in_specs=(rows, P("batch", None), P("batch", None), P(every), P(every, None), P(every, None), P(every),
                  P(every, None), P(every, None), rows),
        out_specs=(rows, rows, P(every), P(every, None), P(every, None), P(every), P(every, None), P(every, None)),
        check_vma=False,
    )
```

```python
import math

import jax
import jax.numpy as jnp
import numpy as np
from jax import lax
from jax.experimental import pallas as pl
from jax.experimental.pallas import tpu as pltpu
from jax.sharding import PartitionSpec as P

HEADS = 12
HEAD_DIM = 128
D = 1536
FF = 6144
DOCS = 6
GROUP = 1024
SHARD = 128
RANK_HEADS = 3
RANK_COLS = 384
EPS = 1e-06
VMEM_LIMIT = 63 * 2**20
BF = jnp.bfloat16
F32 = jnp.float32
MESH = pl.DeviceIdType.MESH


def coords():
    b = lax.axis_index("batch")
    s = lax.axis_index("seq")
    return b // 4, (b // 2) % 2, b % 2, s // 2, s % 2


def dev(y, zl, c, x, zh):
    return (y * 4 + zl * 2 + c, x * 2 + zh)


def x_peers():
    y, zl, c, x, zh = coords()
    return [dev(y, zl, c, (x + k) % 4, zh) for k in (1, 2, 3)]


def y_peers():
    y, zl, c, x, zh = coords()
    return [dev((y + k) % 4, zl, c, x, zh) for k in (1, 2, 3)]


def z_peers():
    y, zl, c, x, zh = coords()
    z = zh * 2 + zl
    return [dev(y, (z + k) % 2, c, x, ((z + k) % 4) // 2) for k in (1, 2, 3)]


def core_peer():
    y, zl, c, x, zh = coords()
    return dev(y, zl, 1 - c, x, zh)


def zh_peer():
    y, zl, c, x, zh = coords()
    return dev(y, zl, c, x, 1 - zh)


class Lines:
    def __init__(self, send, recv):
        self.send, self.recv, self.used = send, recv, 0

    def copy(self, src, dst, peer):
        at = self.used
        self.used += 1
        return pltpu.make_async_remote_copy(
            src, dst, self.send.at[at], self.recv.at[at], device_id=peer, device_id_type=MESH
        )


LO, HI = pl.ds(0, 64), pl.ds(64, 64)


def ring(axis):
    y, zl, c, x, zh = coords()
    if axis == "x":
        return x, x_peers()[0], x_peers()[2]
    if axis == "y":
        return y, y_peers()[0], y_peers()[2]
    return zh * 2 + zl, z_peers()[0], z_peers()[2]


class RingGather:
    def __init__(self, lines, axis, lo, hi):
        self.lines, self.axis, self.lo, self.hi = lines, axis, lo, hi

    def start(self):
        me, nxt, prv = ring(self.axis)
        lo, hi = self.lo(me), self.hi(me)
        self.first = self.lines.copy(lo, lo, nxt)
        self.second = self.lines.copy(hi, hi, prv)
        self.rest = [self.lines.copy(hi, hi, nxt), self.lines.copy(lo, lo, prv)]
        for cp in (self.first, self.second, *self.rest):
            cp.start()

    def on(self):
        me, nxt, prv = ring(self.axis)
        lo, hi = self.lo((me + 3) % 4), self.hi((me + 1) % 4)
        self.first.wait_recv()
        one = self.lines.copy(lo, lo, nxt)
        one.start()
        self.second.wait_recv()
        two = self.lines.copy(hi, hi, prv)
        two.start()
        self.rest += [one, two]

    def near(self):
        for cp in self.rest[:2]:
            cp.wait()
        self.rest = self.rest[2:]

    def finish(self):
        self.first.wait_send()
        self.second.wait_send()
        for cp in self.rest:
            cp.wait()


class RingScatter:
    def __init__(self, lines, axis, lo, hi, got, via):
        self.lines, self.axis, self.lo, self.hi, self.got, self.via = lines, axis, lo, hi, got, via

    def start(self):
        self.start_far()
        self.start_near()

    def start_far(self):
        me, nxt, prv = ring(self.axis)
        far = (me + 2) % 4
        self.far_lo = self.lines.copy(self.lo(far), self.via.at[0], nxt)
        self.far_hi = self.lines.copy(self.hi(far), self.via.at[1], prv)
        self.far_lo.start()
        self.far_hi.start()

    def start_near(self):
        me, nxt, prv = ring(self.axis)
        left, right = (me + 3) % 4, (me + 1) % 4
        self.rest = [
            self.lines.copy(self.hi(right), self.got.at[2], nxt),
            self.lines.copy(self.lo(left), self.got.at[0], prv),
        ]
        for cp in self.rest:
            cp.start()

    def on(self):
        me, nxt, prv = ring(self.axis)
        left, right = (me + 3) % 4, (me + 1) % 4
        via = self.via
        self.far_lo.wait_recv()
        via[0] = (via[0].astype(F32) + self.lo(right)[...].astype(F32)).astype(BF)
        one = self.lines.copy(via.at[0], self.got.at[1], nxt)
        one.start()
        self.far_hi.wait_recv()
        via[1] = (via[1].astype(F32) + self.hi(left)[...].astype(F32)).astype(BF)
        two = self.lines.copy(via.at[1], self.got.at[3], prv)
        two.start()
        self.rest += [one, two]

    def finish(self):
        self.far_lo.wait_send()
        self.far_hi.wait_send()
        for cp in self.rest:
            cp.wait()

    def others(self):
        got = self.got
        return got[0].astype(F32) + got[1].astype(F32), got[2].astype(F32) + got[3].astype(F32)

    def total(self, own):
        return own + jnp.concatenate(self.others(), axis=0)


def gather_x(lines, place):
    return RingGather(lines, "x", lambda i: place(i, LO), lambda i: place(i, HI))


def scatter_x(lines, parts, got, via):
    return RingScatter(lines, "x", lambda i: parts.at[i, LO], lambda i: parts.at[i, HI], got, via)


def one_hot_rows(rows, cols, expand):
    i = lax.broadcasted_iota(jnp.int32, (rows, cols), 0)
    j = lax.broadcasted_iota(jnp.int32, (rows, cols), 1)
    a, p = (j, i) if expand else (i, j)
    return jnp.where((p % 16 < 12) & (p // 16 * 12 + p % 16 == a), 1.0, 0.0).astype(BF)


def pick(matrix, values):
    return jnp.dot(matrix, values, preferred_element_type=F32).astype(BF)


def seq_peers():
    y, zl, c, x, zh = coords()
    s = x * 2 + zh
    found = []
    for k in range(1, 8):
        t = (s + k) % 8
        found.append(dev(y, zl, c, t // 2, t % 2))
    return found


def greet():
    y, _, _, x, _ = coords()
    sem = pltpu.get_barrier_semaphore()
    peers = seq_peers() + y_peers() + z_peers()[::2] + [core_peer()]
    for peer in peers:
        pl.semaphore_signal(sem, inc=1, device_id=peer, device_id_type=MESH)

    @pl.when(x != y)
    def _():
        pl.semaphore_signal(sem, inc=1, device_id=swap_xy(), device_id_type=MESH)

    return len(peers) + jnp.where(x != y, 1, 0)


def swap_xy():
    y, zl, c, x, zh = coords()
    return dev(x, zl, c, y, zh)


def spread(lines, src, dst):
    y, zl, c, x, zh = coords()
    s = x * 2 + zh
    at = lines.used
    lines.used += 4
    sends, arrivals = [], []
    for k in range(4):
        i = (x + k) % 4
        own = (i == x) & (x // 2 == zh)
        cp = pltpu.make_async_remote_copy(
            src.at[i], dst.at[s % 4], lines.send.at[at + k], lines.recv.at[at + s % 4],
            device_id=dev(y, zl, c, i, x // 2), device_id_type=MESH,
        )
        sends.append((cp, own))
    for j in range(4):
        own = (x // 2 == zh) & (s % 4 == j)
        cp = pltpu.make_async_remote_copy(
            src.at[j], dst.at[j], lines.send.at[at], lines.recv.at[at + j],
            device_id=core_peer(), device_id_type=MESH,
        )
        arrivals.append((cp, own))
    return sends, arrivals, (x // 2 == zh), x, s % 4


def gather_home(lines, src, dst):
    y, zl, c, x, zh = coords()
    s = x * 2 + zh
    at = lines.used
    lines.used += 4
    sends, arrivals = [], []
    for k in range(4):
        i = (s + k) % 4
        t = 4 * zh + i
        own = t == s
        cp = pltpu.make_async_remote_copy(
            src.at[i], dst.at[x], lines.send.at[at + k], lines.recv.at[at + x],
            device_id=dev(y, zl, c, t // 2, t % 2), device_id_type=MESH,
        )
        sends.append((cp, own))
    for j in range(4):
        own = (x // 2 == zh) & (x == j)
        cp = pltpu.make_async_remote_copy(
            src.at[j], dst.at[j], lines.send.at[at], lines.recv.at[at + j],
            device_id=core_peer(), device_id_type=MESH,
        )
        arrivals.append((cp, own))
    return sends, arrivals, (x // 2 == zh), s % 4, x


def start_all(plan, src, dst):
    sends, _, mine, from_slot, to_slot = plan
    for cp, own in sends:
        pl.when(jnp.logical_not(own))(cp.start)

    @pl.when(mine)
    def _():
        dst[to_slot] = src[from_slot]


def wait_all(plan):
    sends, arrivals = plan[:2]
    for cp, own in arrivals:
        pl.when(jnp.logical_not(own))(cp.wait_recv)
    for cp, own in sends:
        pl.when(jnp.logical_not(own))(cp.wait_send)


class Gather:
    def __init__(self, lines, full, rows, z_first, y_inner=False, columns=None):
        self.lines, self.full, self.rows, self.z_first, self.y_inner = lines, full, rows, z_first, y_inner
        self.columns = pl.ds(0, full.shape[-1]) if columns is None else columns
        self.pending = []

    def _at(self, y, zl, c, rows):
        place = (zl, c, y) if self.y_inner else (y, zl, c)
        return self.full.at[(*place, rows, self.columns)]

    def _send(self, src, peers):
        copies = [self.lines.copy(src, src, p) for p in peers]
        for cp in copies:
            cp.start()
        self.pending = copies

    def near(self):
        y, zl, c, _, zh = coords()
        mine = self._at(y, zl, c, pl.ds(zh * self.rows, self.rows))
        self._send(mine, z_peers() if self.z_first else y_peers())

    def wide(self):
        self.wait()
        y, zl, c, _, zh = coords()
        if self.z_first:
            rows = pl.ds(0, 2 * self.rows)
            self.ring = RingGather(
                self.lines, "y", lambda i: self._at(i, 0, c, rows), lambda i: self._at(i, 1, c, rows)
            )
        else:
            rows = lambda i: pl.ds(i // 2 * self.rows, self.rows)
            self.ring = RingGather(
                self.lines, "z", lambda i: self._at(pl.ds(0, 2), i % 2, c, rows(i)),
                lambda i: self._at(pl.ds(2, 2), i % 2, c, rows(i)),
            )
        self.ring.start()

    def on(self):
        self.ring.on()

    def cores(self):
        self.ring.finish()
        c = coords()[2]
        self._send(self._at(slice(None), slice(None), c, pl.ds(0, 2 * self.rows)), [core_peer()])

    def wait(self):
        for cp in self.pending:
            cp.wait()
        self.pending = []


class Scatter:
    def __init__(self, lines, part, bufs, rows, y_first, y_inner=False, columns=None):
        self.lines, self.part = lines, part
        self.half, self.got, self.via, self.wide, self.wide_in = bufs
        self.rows, self.y_first, self.y_inner, self.pending = rows, y_first, y_inner, []
        self.columns = pl.ds(0, part.shape[-1]) if columns is None else columns

    def wait(self):
        for cp in self.pending:
            cp.wait()
        self.pending = []

    def _start(self, copies):
        for cp in copies:
            cp.start()
        self.pending = copies

    def cores(self):
        c = coords()[2]
        rows = pl.ds(0, 2 * self.rows)
        place = (slice(None), 1 - c, slice(None)) if self.y_inner else (slice(None), slice(None), 1 - c)
        self._start([self.lines.copy(self.part.at[(*place, rows, self.columns)], self.half, core_peer())])

    def _block(self, side, i):
        if not self.y_first:
            rows, pair = pl.ds(i // 2 * self.rows, self.rows), pl.ds(2 * side, 2)
            return self.half.at[i % 2, pair, rows] if self.y_inner else self.half.at[pair, i % 2, rows]
        return self.half.at[side, i] if self.y_inner else self.half.at[i, side]

    def first(self):
        self.wait()
        c, inner = coords()[2], self.half.shape[1]

        @pl.loop(0, 8)
        def _(i):
            a, b = i // inner, i % inner
            place = (a, c, b) if self.y_inner else (a, b, c)
            both = self.part[(*place, slice(None), self.columns)].astype(F32) + self.half[a, b].astype(F32)
            self.half[a, b] = both.astype(BF)

        self.ring = RingScatter(
            self.lines, "y" if self.y_first else "z", lambda i: self._block(0, i), lambda i: self._block(1, i),
            self.got, self.via,
        )
        self.ring.start()

    def on(self):
        self.ring.on()

    def second(self):
        self.ring.finish()
        me = ring("y" if self.y_first else "z")[0]
        for side, others in enumerate(self.ring.others()):
            self.wide[side] = (self._block(side, me)[...].astype(F32) + others).astype(BF)
        copies = []
        for k in (1, 2, 3):
            peer = (z_peers if self.y_first else y_peers)()[k - 1]
            copies.append(self.lines.copy(self._piece(k), self.wide_in.at[k - 1], peer))
        self._start(copies)

    def _piece(self, k):
        y, zl, c, _, zh = coords()
        if self.y_first:
            zz = (zh * 2 + zl + k) % 4
            return self.wide.at[zz % 2, pl.ds(zz // 2 * self.rows, self.rows)]
        yy = (y + k) % 4
        return self.wide.at[yy // 2, yy % 2]

    def total(self):
        self.wait()
        total = self._piece(0)[...].astype(F32)
        for k in range(3):
            total += self.wide_in[k].astype(F32)
        return total


class Pair:
    def __init__(self, *parts):
        self.parts = parts

    def __getattr__(self, step):
        return lambda: [getattr(p, step)() for p in self.parts]

    def sums(self):
        return jnp.concatenate([p.total().astype(BF) for p in self.parts], axis=1)


def gather_both(lines, full, rows, split, width, y_inner=False):
    return Pair(
        Gather(lines, full, rows, False, y_inner, pl.ds(split, width - split)),
        Gather(lines, full, rows, True, y_inner, pl.ds(0, split)),
    )


def scatter_both(lines, part, bufs, rows, split, width, y_inner=False):
    n = len(bufs) // 2
    return Pair(
        Scatter(lines, part, bufs[:n], rows, False, y_inner, pl.ds(0, split)),
        Scatter(lines, part, bufs[n:], rows, True, y_inner, pl.ds(split, width - split)),
    )


def scatter_scratch(rows, split, width, y_inner=False):
    found = []
    for n, y_first in ((split, False), (width - split, True)):
        half = (2, 4, 2 * rows, n) if y_inner else (4, 2, 2 * rows, n)
        block = (2 * rows, n) if y_first else (2, rows, n)
        found += [pltpu.VMEM(s, BF) for s in (half, (4, *block), (2, *block), (2, *block), (3, rows, n))]
    return found


def dot(a, b):
    return jnp.dot(a, b, preferred_element_type=F32)


def dot_nt(a, b):
    return lax.dot_general(a, b, (((1,), (1,)), ((), ())), preferred_element_type=F32)


def dot_tn(a, b):
    return lax.dot_general(a, b, (((0,), (0,)), ((), ())), preferred_element_type=F32)


def normalize(values):
    r = lax.rsqrt(jnp.mean(values * values, axis=-1, keepdims=True) + EPS)
    return r, values * r


def rms_back(grad, values):
    r, hat = normalize(values)
    return r * (grad - hat * jnp.mean(grad * hat, axis=-1, keepdims=True))


def cos_sin(table):
    other = pltpu.roll(table, 64, 1)
    low = lax.broadcasted_iota(jnp.int32, table.shape, 1) < 64
    return jnp.where(low, table, other), jnp.where(low, -other, table)


def turn(v, cos, sin):
    return v * cos + pltpu.roll(v, 64, 1) * sin


def turn_back(v, cos, sin):
    return v * cos - pltpu.roll(v, 64, 1) * sin


GELU_A, GELU_B = math.sqrt(2.0 / math.pi), 0.044715


def gelu_both(v):
    square = v * v
    t = jnp.tanh(GELU_A * v * (1.0 + GELU_B * square))
    half = 0.5 * (1.0 + t)
    return v * half, half + 0.5 * v * (1.0 - t * t) * (GELU_A * (1.0 + 3.0 * GELU_B * square))


def cols(i, n):
    return pl.ds(pl.multiple_of(i * n, n), n)


NAMES = (
    "full_q", "full_u", "full_d", "full_o", "got_q", "got_u", "src_q", "src_u", "src_o",
    "normed", "q_ref", "k_ref", "v_ref", "p0", "p1", "p2", "p3",
    "att", "att_grad", "middle", "wo", "ntwo", "up_grad", "hidden", "pre_grad", "branch", "part_a",
    "got_a", "via_a", "got_b", "via_b", "swap_in", "dk_t", "dv_t",
    *(f"s{w}{k}" for w in "qudo" for k in range(10)), "send", "recv",
    "tokens", "qkv", "grad_in", "up", "out_w", "down", "angles", "load",
)


def scratch_list():
    V = pltpu.VMEM
    block = V((4, 128, D), BF)
    got, via = V((4, 64, D), BF), V((2, 64, D), BF)
    kv = V((3, 4, 2, 128, 128), BF)
    shapes = [V((4, 2, 2, 96, 1152), BF), V((4, 2, 2, 96, D), BF), V((2, 2, 4, 96, D), BF), V((2, 2, 4, 32, D), BF)]
    shapes += [V((4, 16, 1152), BF), V((4, 16, D), BF)] * 2 + [V((16, D), BF)]
    shapes += [V((4, 2, 128, D), BF), V((3, 4, 128, 128), BF), kv, kv]
    shapes += [V((3, 128, 256 * (i + 1)), BF) for i in range(4)]
    shapes += [V((4, 128, RANK_COLS), BF), V((4, 128, RANK_COLS), BF), V((128, D), F32), V((RANK_COLS, D), BF)]
    shapes += [block] * 6
    shapes += [got, via] * 2 + [V((128, D), BF)]
    shapes += [V((128, GROUP), F32), V((128, GROUP), F32)]
    shapes += scatter_scratch(48, RANK_COLS, 1152) + scatter_scratch(48, 768, D)
    shapes += scatter_scratch(48, 768, D, True) + scatter_scratch(16, 768, D, True)
    shapes += [pltpu.SemaphoreType.DMA((300,)), pltpu.SemaphoreType.DMA((300,))]
    rows = V((128, D), BF)
    shapes += [rows, V((12, 3 * D), BF), rows, V((12, FF), BF), V((12, D), BF), V((48, D), BF)]
    shapes += [V((4, 2, 128, 128), F32), pltpu.SemaphoreType.DMA((7,))]
    assert len(shapes) == len(NAMES)
    return shapes


class Refs:
    pass


def column(row):
    n = row.shape[1]
    same = lax.broadcasted_iota(jnp.int32, (n, n), 0) == lax.broadcasted_iota(jnp.int32, (n, n), 1)
    return jnp.sum(jnp.where(same, row, 0.0), axis=1, keepdims=True)


def as_row(col):
    n = col.shape[0]
    same = lax.broadcasted_iota(jnp.int32, (n, n), 0) == lax.broadcasted_iota(jnp.int32, (n, n), 1)
    return jnp.sum(jnp.where(same, col, 0.0), axis=0, keepdims=True)


def sixteen(rows):
    return jnp.concatenate([rows, jnp.zeros((4, rows.shape[1]), rows.dtype)], axis=0).astype(BF)


def documents(lengths, levels, positions):
    start, width = jnp.zeros_like(positions), jnp.zeros_like(positions)
    first = 0
    for d in range(DOCS):
        level = levels[0, d]
        wide = jnp.where(level == 0, FF // 8, jnp.where(level == 1, FF // 4, jnp.where(level == 2, FF // 2, FF)))
        inside = positions >= first
        start = jnp.where(inside, first, start)
        width = jnp.where(inside, wide, width)
        first = first + lengths[0, d]
    return start, width


def layer_kernel(
    lengths, levels, gain_one, gain_two, tokens_in, grad_in_in, qkv_in, out_w_in, up_in, down_in, angles_in,
    block_out, grad_input, out_q, out_u, out_d, out_o, *scratch
):
    g = Refs()
    for name, ref in zip(NAMES, scratch):
        setattr(g, name, ref)
    bufs = lambda w: [getattr(g, f"s{w}{k}") for k in range(10)]
    y, zl, c, x, zh = coords()
    lines = Lines(g.send, g.recv)
    scale = HEAD_DIM**-0.5
    greetings = greet()

    tokens, grad_in, qkv, out_w, up, down, angles = g.tokens, g.grad_in, g.qkv, g.out_w, g.up, g.down, g.angles
    pairs = [
        (tokens_in, tokens), (qkv_in, qkv), (grad_in_in, grad_in), (up_in, up), (out_w_in, out_w), (down_in, down),
        (angles_in, angles),
    ]
    loads = [pltpu.make_async_copy(a, b, g.load.at[k]) for k, (a, b) in enumerate(pairs)]
    for cp in loads:
        cp.start()
    loads[0].wait()
    g.normed[x, zh] = normalize(tokens[...].astype(F32))[1].astype(BF)
    one, two = column(gain_one[...].astype(F32)), column(gain_two[...].astype(F32))
    loads[1].wait()
    for i in range(4):
        for j in range(3):
            at = j * D + i * RANK_COLS
            g.src_q[i, :, j * RANK_COLS : (j + 1) * RANK_COLS] = sixteen(qkv[:, at : at + RANK_COLS].astype(F32) * one)
    for cp in loads[2:5]:
        cp.wait()
    g.up_grad[x] = grad_in[...]
    for i in range(4):
        g.src_u[i] = sixteen(up[:, i * D : (i + 1) * D].astype(F32) * two)
    g.src_o[...] = sixteen(out_w[...].astype(F32))
    for cp in loads[5:]:
        cp.wait()
    pl.semaphore_wait(pltpu.get_barrier_semaphore(), greetings)

    ring_one = gather_x(lines, lambda i, h: g.normed.at[i, zh, h])
    ring_two = gather_x(lines, lambda i, h: g.normed.at[i, 1 - zh, h])
    swap = lines.copy(g.normed.at[x, zh], g.normed.at[x, zh], zh_peer())
    plan_q = spread(lines, g.src_q, g.got_q)
    start_all(plan_q, g.src_q, g.got_q)
    swap_o = lines.copy(g.src_o, g.full_o.at[zl, c, x, pl.ds(zh * 16, 16)], swap_xy())
    swap_d = lines.copy(down, g.full_d.at[zl, c, x, pl.ds(zh * 48, 48)], swap_xy())
    swap.start()
    ring_one.start()
    pl.when(x != y)(swap_o.start)
    rows = one_hot_rows(48, 64, False)
    wait_all(plan_q)
    g.full_q[y, zl, c, pl.ds(zh * 48, 48)] = pick(rows, g.got_q[...].reshape(64, 1152))
    gather_q = gather_both(lines, g.full_q, 48, 256, 1152)
    gather_o = Gather(lines, g.full_o, 16, True, True)
    gather_u = gather_both(lines, g.full_u, 48, 768, D)
    gather_d = gather_both(lines, g.full_d, 48, 768, D, True)
    gather_q.near()

    @pl.when(x == y)
    def _():
        g.full_o[zl, c, x, pl.ds(zh * 16, 16)] = g.src_o[...]
        g.full_d[zl, c, x, pl.ds(zh * 48, 48)] = down[...]

    ring_one.on()
    gather_q.wide()
    pl.when(x != y)(swap_d.start)
    swap.wait_recv()
    ring_two.start()
    gather_q.on()
    pl.when(x != y)(swap_o.wait)
    gather_o.near()
    ring_two.on()
    plan_u = spread(lines, g.src_u, g.got_u)
    start_all(plan_u, g.src_u, g.got_u)
    gather_q.cores()
    gather_o.wide()
    pl.when(x != y)(swap_d.wait)
    gather_d.near()
    ring_one.finish()
    gather_q.wait()

    def project(zz, own_half):
        block = g.normed[:, zz].reshape(512, D)
        cos_b, sin_b = cos_sin(angles[:, zz].reshape(512, 128))
        for j in range(0 if own_half else 1, 3):
            made = dot(block, g.full_q[:, :, :, :, j * RANK_COLS : (j + 1) * RANK_COLS].reshape(D, RANK_COLS))
            for h in range(RANK_HEADS):
                head = made[:, h * 128 : (h + 1) * 128]
                if j < 2:
                    head = turn(head, cos_b, sin_b)
                head = head.astype(BF).reshape(4, 128, 128)
                if j == 0:
                    g.q_ref[h] = head
                elif j == 1:
                    g.k_ref[h, :, zz] = head
                else:
                    g.v_ref[h, :, zz] = head

    project(zh, True)
    gather_o.on()
    ring_two.finish()
    swap.wait_send()
    ring_up = gather_x(lines, lambda i, h: g.up_grad.at[i, h])
    ring_up.start()
    project(1 - zh, False)
    gather_d.wide()
    wait_all(plan_u)
    g.full_u[y, zl, c, pl.ds(zh * 48, 48)] = pick(rows, g.got_u[...].reshape(64, D))
    gather_u.near()
    gather_o.cores()

    probs = [g.p0, g.p1, g.p2, g.p3]

    def attend(h):
        for i in range(4):
            n = 256 * (i + 1)
            keys = g.k_ref[h, : i + 1].reshape(n, 128)
            values = g.v_ref[h, : i + 1].reshape(n, 128)
            scores = dot_nt(g.q_ref[h, i], keys) * scale
            base = (2 * i + zh) * 128
            q_at = base + lax.broadcasted_iota(jnp.int32, (128, n), 0)
            k_at = lax.broadcasted_iota(jnp.int32, (128, n), 1)
            first = documents(lengths, levels, base + lax.broadcasted_iota(jnp.int32, (128, 1), 0))[0]
            scores = jnp.where((k_at <= q_at) & (k_at >= first), scores, -1e30)
            e = jnp.exp(scores - jnp.max(scores, axis=-1, keepdims=True))
            p = (e * (1.0 / jnp.sum(e, axis=-1, keepdims=True))).astype(BF)
            probs[i][h] = p
            g.att[i, :, pl.ds(pl.multiple_of(h * 128, 128), 128)] = dot(p, values).astype(BF)

    attend(0)
    ring_up.on()
    attend(1)
    gather_d.on()
    attend(2)
    gather_o.wait()
    g.wo[...] = pick(one_hot_rows(RANK_COLS, 512, False), g.full_o[...].reshape(512, D))

    def to_parts(parts, left, right_of, transposed, tiles):
        n = D // tiles

        @pl.loop(0, tiles)
        def _(t):
            right = right_of(t)
            made = dot_nt(left(), right) if transposed else dot(left(), right)
            parts[:, :, cols(t, n)] = made.astype(BF).reshape(4, 128, n)

    to_parts(g.part_a, lambda: g.att[...].reshape(512, RANK_COLS), lambda t: g.wo[:, cols(t, 512)], False, 3)
    ring_a = scatter_x(lines, g.part_a, g.got_a, g.via_a)
    ring_a.start()
    gather_u.wide()
    gather_d.cores()

    ring_a.on()
    gather_u.on()
    ring_up.finish()
    gather_d.wait()
    up_all = lambda: g.up_grad[...].reshape(512, D)
    to_parts(g.pre_grad, up_all, lambda t: g.full_d[t].reshape(768, D), True, 2)
    gather_u.cores()
    ring_a.finish()
    g.middle[...] = ring_a.total(tokens[...].astype(F32) + g.part_a[x].astype(F32))
    g.ntwo[x] = normalize(g.middle[...])[1].astype(BF)
    ring_n = gather_x(lines, lambda i, h: g.ntwo.at[i, h])
    ring_n.start()

    def full_rows(ref, t):
        return ref[pl.ds(t * 2, 2)].reshape(768, ref.shape[-1])

    def full_cols(ref, t, n):
        return ref[:, :, :, :, cols(t, n)].reshape(D, n)

    gather_u.wait()

    def feed_forward(blocks, tile):
        rows = 128 * len(blocks)
        at = [(2 * i + zh) * 128 + lax.broadcasted_iota(jnp.int32, (128, 1), 0) for i in blocks]
        width = jnp.concatenate([documents(lengths, levels, p)[1] for p in at], axis=0)

        @pl.loop(0, D // tile)
        def _(t):
            normed_rows = jnp.concatenate([g.ntwo[i] for i in blocks], axis=0)
            pre = dot(normed_rows, full_cols(g.full_u, t, tile))
            unit = x * D + t * tile + lax.broadcasted_iota(jnp.int32, (rows, tile), 1)
            mask = unit < width
            act, slope = gelu_both(pre)
            act = jnp.where(mask, act, 0.0).astype(BF)
            slope = jnp.where(mask, slope, 0.0)
            for k, i in enumerate(blocks):
                own = slice(128 * k, 128 * (k + 1))
                g.hidden[i, :, cols(t, tile)] = act[own]
                back = g.pre_grad[i, :, cols(t, tile)].astype(F32)
                g.pre_grad[i, :, cols(t, tile)] = (slope[own] * back).astype(BF)

        @pl.loop(0, 2)
        def _(t):
            pre_rows = jnp.concatenate([g.pre_grad[i] for i in blocks], axis=0)
            made = dot_nt(pre_rows, full_rows(g.full_u, t)).astype(BF)
            for k, i in enumerate(blocks):
                g.part_a[i, :, cols(t, 768)] = made[128 * k : 128 * (k + 1)]

    feed_forward([x], 512)
    ring_n.on()
    ring_n.near()
    ring_b = scatter_x(lines, g.part_a, g.got_b, g.via_b)
    feed_forward([(x + 3) % 4, (x + 1) % 4], 256)
    ring_b.start_near()
    ring_n.finish()
    feed_forward([(x + 2) % 4], 512)
    ring_b.start_far()
    pre_all = lambda: g.pre_grad[...].reshape(512, D)

    def weight_grad(full, left_of, right):
        @pl.loop(0, 4)
        def _(t):
            made = dot_tn(left_of(t), right()).astype(BF)
            if full.shape[0] == 4:
                full[t] = made.reshape(full.shape[1:])
            else:
                full[t // 2, t % 2] = made.reshape(full.shape[2:])

    weight_grad(g.full_u, lambda t: g.ntwo[:, :, cols(t, 384)].reshape(512, 384), pre_all)
    scatter_u = scatter_both(lines, g.full_u, bufs("u"), 48, 768, D)
    scatter_u.cores()
    ring_b.on()
    to_parts(g.pre_grad, lambda: g.hidden[...].reshape(512, D), lambda t: full_cols(g.full_d, t, 512), False, 3)
    scatter_u.first()
    ring_b.finish()

    grad_input[...] = grad_in[...].astype(F32) + rms_back(ring_b.total(g.part_a[x].astype(F32)), g.middle[...])
    g.branch[x] = grad_input[...].astype(BF)
    ring_g = gather_x(lines, lambda i, h: g.branch.at[i, h])
    ring_g.start()
    weight_grad(g.full_d, lambda t: g.hidden[:, :, cols(t, 384)].reshape(512, 384), up_all)
    scatter_d = scatter_both(lines, g.full_d, bufs("d"), 48, 768, D, True)
    scatter_d.cores()
    padded = pick(g.att[...].reshape(512, RANK_COLS), one_hot_rows(RANK_COLS, 512, False))
    g.hidden[:, :, :512] = padded.reshape(4, 128, 512)
    scatter_u.on()
    ring_g.on()
    scatter_d.first()
    ring_g.finish()
    ring_c = scatter_x(lines, g.pre_grad, g.up_grad.at[:, LO], g.up_grad.at[pl.ds(0, 2), HI])
    ring_c.start()

    branch_all = lambda: g.branch[...].reshape(512, D)
    scatter_u.second()
    g.att_grad[...] = dot_nt(branch_all(), g.wo[...]).astype(BF).reshape(4, 128, RANK_COLS)

    def attend_back(h):
        at = pl.ds(pl.multiple_of(h * 128, 128), 128)
        g.dk_t[...] = jnp.zeros_like(g.dk_t)
        g.dv_t[...] = jnp.zeros_like(g.dv_t)
        for i in range(4):
            n = 256 * (i + 1)
            keys = g.k_ref[h, : i + 1].reshape(n, 128)
            values = g.v_ref[h, : i + 1].reshape(n, 128)
            queries = g.q_ref[h, i]
            p = probs[i][h]
            grad = g.att_grad[i, :, at]
            delta = jnp.sum(grad.astype(F32) * g.att[i, :, at].astype(F32), axis=-1, keepdims=True)
            ds = (p.astype(F32) * (dot_nt(grad, values) - delta)).astype(BF)
            dq = dot(ds, keys) * scale
            g.dk_t[:, :n] += dot(queries.T, ds)
            g.dv_t[:, :n] += dot(grad.T, p)
            g.q_ref[h, i] = turn_back(dq, *cos_sin(angles[i, zh])).astype(BF)
        dk = g.dk_t[...].T * scale
        dk = turn_back(dk, *cos_sin(angles[...].reshape(GROUP, 128)))
        g.k_ref[h] = dk.astype(BF).reshape(4, 2, 128, 128)
        g.v_ref[h] = g.dv_t[...].T.astype(BF).reshape(4, 2, 128, 128)

    attend_back(0)
    scatter_d.on()
    pl.loop(1, RANK_HEADS)(attend_back)
    ring_c.on()

    def side(ref, zz):
        return [ref[h, :, zz].reshape(512, 128) for h in range(RANK_HEADS)]

    def first_parts(parts, zz, own_half):
        def left():
            pieces = side(g.k_ref, zz) + side(g.v_ref, zz)
            if own_half:
                pieces = [g.q_ref[h].reshape(512, 128) for h in range(RANK_HEADS)] + pieces
            return jnp.concatenate(pieces, axis=1)

        n = 1152 if own_half else 768
        to_parts(parts, left, lambda t: g.full_q[pl.ds(t * 2, 2), :, :, :, 1152 - n :].reshape(768, n), True, 2)

    first_parts(g.part_a, 1 - zh, False)
    ring_e = scatter_x(lines, g.part_a, g.got_a, g.via_a)
    ring_e.start()
    weight_grad(g.full_o, lambda t: g.hidden[:, :, cols(t, 128)].reshape(512, 128), branch_all)
    scatter_o = scatter_both(lines, g.full_o, bufs("o"), 16, 768, D, True)
    scatter_o.cores()
    scatter_q = scatter_both(lines, g.full_u, bufs("q"), 48, RANK_COLS, 1152)
    part_q, part_kv = scatter_q.parts
    dq_all = lambda: jnp.concatenate([g.q_ref[h].reshape(512, 128) for h in range(RANK_HEADS)], axis=1)
    dkv_all = lambda: jnp.concatenate(
        [r[h].reshape(GROUP, 128) for r in (g.k_ref, g.v_ref) for h in range(RANK_HEADS)], axis=1
    )

    @pl.loop(0, 4)
    def _(t):
        every = g.normed[:, :, :, cols(t, 384)].reshape(GROUP, 384)
        g.full_u[t, :, :, :, RANK_COLS:1152] = dot_tn(every, dkv_all()).astype(BF).reshape(2, 2, 96, 768)

    part_kv.cores()
    scatter_o.first()
    scatter_d.second()
    spread_rows = one_hot_rows(64, 48, True)
    g.got_u[...] = pick(spread_rows, scatter_u.sums()).reshape(4, 16, D)
    plan_u = gather_home(lines, g.got_u, out_u)
    start_all(plan_u, g.got_u, out_u)

    @pl.loop(0, 4)
    def _(t):
        mine = g.normed[:, zh, :, cols(t, 384)].reshape(512, 384)
        g.full_u[t, :, :, :, :RANK_COLS] = dot_tn(mine, dq_all()).astype(BF).reshape(2, 2, 96, RANK_COLS)

    part_q.cores()
    part_kv.first()
    ring_e.on()
    part_q.first()
    first_parts(g.ntwo, zh, True)
    ring_f = scatter_x(lines, g.ntwo, g.got_b, g.via_b)
    ring_f.start()
    scatter_o.on()
    scatter_q.on()
    scatter_o.second()
    g.down[...] = scatter_d.sums()
    home_d = lines.copy(g.down, out_d, swap_xy())
    home_o = lines.copy(g.src_o, out_o, swap_xy())
    pl.when(x != y)(home_d.start)
    ring_e.finish()
    g.grad_in[...] = ring_e.total(g.part_a[x].astype(F32)).astype(BF)
    scatter_q.second()
    back = lines.copy(g.grad_in, g.swap_in, zh_peer())
    back.start()
    ring_f.on()
    ring_c.finish()
    block_out[...] = ring_c.total(g.middle[...] + g.pre_grad[x].astype(F32)).astype(BF)
    g.src_o[...] = scatter_o.sums()
    pl.when(x != y)(home_o.start)

    g.got_q[...] = pick(spread_rows, scatter_q.sums()).reshape(4, 16, 1152)
    plan_q = gather_home(lines, g.got_q, out_q)
    start_all(plan_q, g.got_q, out_q)
    ring_f.finish()
    back.wait()
    h_one = ring_f.total(g.ntwo[x].astype(F32)) + g.swap_in[...].astype(F32)
    grad_input[...] += rms_back(h_one, tokens[...].astype(F32))

    @pl.when(x == y)
    def _():
        out_o[...] = g.src_o[...]
        out_d[...] = g.down[...]

    wait_all(plan_u)

    @pl.when(x != y)
    def _():
        home_d.wait()
        home_o.wait()

    wait_all(plan_q)


def finish_kernel(
    block, grad, got_q, got_u, got_d, got_o, qkv, up, gain_one, gain_two,
    block_out, grad_input, d_gain_one, d_qkv, d_out, d_gain_two, d_up, d_down
):
    block_out[...] = block[...]
    grad_input[...] = grad[...]
    d_down[...] = got_d[...].astype(F32)
    d_out[...] = got_o[:12].astype(F32)
    one, two = column(gain_one[...].astype(F32)), column(gain_two[...].astype(F32))
    sum_one = sum_two = jnp.zeros((12, 1), F32)
    for i in range(4):
        for j in range(3):
            raw = got_q[i, :12, j * RANK_COLS : (j + 1) * RANK_COLS].astype(F32)
            at = j * D + i * RANK_COLS
            sum_one += jnp.sum(raw * qkv[:, at : at + RANK_COLS].astype(F32), axis=1, keepdims=True)
            d_qkv[:, at : at + RANK_COLS] = raw * one
        raw = got_u[i, :12].astype(F32)
        sum_two += jnp.sum(raw * up[:, i * D : (i + 1) * D].astype(F32), axis=1, keepdims=True)
        d_up[:, i * D : (i + 1) * D] = raw * two
    d_gain_one[...] = as_row(sum_one)
    d_gain_two[...] = as_row(sum_two)


def tables():
    inverse = np.exp(np.arange(64) * (-2.0 * math.log(10000.0) / HEAD_DIM))
    angles = np.arange(GROUP)[:, None] * inverse[None, :]
    return np.concatenate([np.cos(angles), np.sin(angles)], axis=1).astype(np.float32).reshape(4, 2, 128, 128)


def shapes_of(pairs):
    return [jax.ShapeDtypeStruct(s, t) for s, t in pairs]


def per_device(
    block_input, doc_lengths, ffn_levels, attn_gain, qkv_weight, out_weight, ffn_gain, up_weight, down_weight, grad_output
):
    vmem = pl.BlockSpec(memory_space=pltpu.VMEM)
    smem = pl.BlockSpec(memory_space=pltpu.SMEM)
    gain_one, gain_two = attn_gain.reshape(1, 12), ffn_gain.reshape(1, 12)
    outs = [((128, D), BF), ((128, D), F32), ((4, 16, 1152), BF), ((4, 16, D), BF), ((48, D), BF), ((16, D), BF)]
    made = pl.pallas_call(
        layer_kernel,
        out_shape=shapes_of(outs),
        in_specs=[smem] * 2 + [vmem] * 2 + [pl.BlockSpec(memory_space=pl.ANY)] * 7,
        out_specs=[vmem] * len(outs),
        scratch_shapes=scratch_list(),
        compiler_params=pltpu.CompilerParams(collective_id=0, has_side_effects=True, vmem_limit_bytes=VMEM_LIMIT),
        name="layer_kernel",
    )(
        doc_lengths, ffn_levels, gain_one, gain_two, block_input[0], grad_output[0], qkv_weight, out_weight, up_weight,
        down_weight, jnp.asarray(tables()),
    )
    outs = [((128, D), BF), ((128, D), F32), ((1, 12), F32), ((12, 3 * D), F32), ((12, D), F32), ((1, 12), F32)]
    outs += [((12, FF), F32), ((48, D), F32)]
    block, grad, d_gain_one, d_qkv, d_out, d_gain_two, d_up, d_down = pl.pallas_call(
        finish_kernel,
        out_shape=shapes_of(outs),
        in_specs=[vmem] * 10,
        out_specs=[vmem] * len(outs),
        compiler_params=pltpu.CompilerParams(vmem_limit_bytes=VMEM_LIMIT),
        name="finish_kernel",
    )(*made, qkv_weight, up_weight, gain_one, gain_two)
    return block[None], grad[None], d_gain_one.reshape(12), d_qkv, d_out, d_gain_two.reshape(12), d_up, d_down


def solution(mesh):
    rows = P("batch", "seq", None)
    every = ("batch", "seq")
    return jax.shard_map(
        per_device,
        mesh=mesh,
        in_specs=(rows, P("batch", None), P("batch", None), P(every), P(every, None), P(every, None), P(every),
                  P(every, None), P(every, None), rows),
        out_specs=(rows, rows, P(every), P(every, None), P(every, None), P(every), P(every, None), P(every, None)),
        check_vma=False,
    )
```
